32 devices in a mesh: band: 2 (over x), pw: 16 (over z, y, core).
Axes of the slice: x: 2, y: 2, z: 4, core: 2. Of those that a mesh axis runs over, the one named last changes fastest.
Arguments:
- basis_re: float32 [8, 2, 2, 4096], P(None, None, 'band', 'pw'), may hold values from -24 to 24
- basis_im: float32 [8, 2, 2, 4096], P(None, None, 'band', 'pw'), may hold values from -24 to 24
- potential: float32 [192, 192, 192], P('pw'), may hold values from -15 to 15
- kinetic: float32 [2, 4096], P(None, 'pw'), may hold values from 0 to 30
- form_factors: float32 [8, 2, 4096], P(None, None, 'pw'), may hold values from -12 to 12
- channel_strength: float32 [8], replicated, may hold values from -4 to 4
- sphere_map: int32 [2, 4096], P(None, 'pw'), may hold values from 0 to 1535, as said below
- column_map: int32 [128], replicated, may hold values from 0 to 36863, as said below
- atom_sites: int32 [3, 512], replicated, may hold values from 0 to 191
Outputs:
- next_re: float32 [2, 2, 4096], P(None, 'band', 'pw')
- next_im: float32 [2, 2, 4096], P(None, 'band', 'pw')
- coeffs_re: float32 [8, 2, 2], replicated
- coeffs_im: float32 [8, 2, 2], replicated
- chol_re: float32 [2, 2], replicated
- chol_im: float32 [2, 2], replicated
The draws below stay inside these ranges and needn't reach their ends.
Inputs may be any that keep to these rules, and one draw needn't show every extreme that they name: `sphere_map`: within each group of 256 consecutive values of the second index, the entries over both indices are distinct. `column_map`: all entries are distinct.
All inputs are finite; a program needn't handle non-finite values.
Results may differ from the reference program's by a relative error of at most 0.0015.
The reference program's roundings to bfloat16 on the way count: a program that leaves them out, or rounds other values in their place, can miss the bound.
Values sent between devices are 32-bit elements; how exact they have to be, the bound alone decides.
A program may use at most 128 MiB of HBM per device.

```python
import math
import jax
import jax.numpy as jnp
from jax import lax

GRID = 192
ROWS_DEV = 256
BLOCKS = 8
ATOMS = 512
CHANNELS = 8
SLAB = 2
PW_SUB = 4096
PWAVES = 8192
COL_DEV = 8
COLUMNS = 128
N_BAND = 2


def pick_distinct(key, span, count):
    middle = jax.random.permutation(key, span - 2)[:count - 2].astype(jnp.int32) + 1
    chosen = jnp.concatenate([jnp.array([0, span - 1], dtype=jnp.int32), middle])
    return chosen[jax.random.permutation(jax.random.fold_in(key, 5), count)]


def band_scales(key):
    low = math.log(0.4)
    high = math.log(4.0)
    return jnp.exp(jax.random.uniform(jax.random.fold_in(key, 97), (1, SLAB, 1, 1), jnp.float32, low, high))


def draw_basis_re(key, part):
    scales = band_scales(key)
    key = jax.random.fold_in(key, 1)
    shape = (BLOCKS, SLAB, PWAVES // PW_SUB, PW_SUB)
    own_key, shared_key = jax.random.split(key)
    noise = jnp.clip(jax.random.normal(own_key, shape, jnp.float32), -4.0, 4.0)
    common = 0.5 * jnp.clip(jax.random.normal(shared_key, (1,) + shape[1:], jnp.float32), -4.0, 4.0)
    return scales * (noise + common)


def draw_basis_im(key, part):
    scales = band_scales(key)
    key = jax.random.fold_in(key, 2)
    shape = (BLOCKS, SLAB, PWAVES // PW_SUB, PW_SUB)
    own_key, shared_key = jax.random.split(key)
    noise = jnp.clip(jax.random.normal(own_key, shape, jnp.float32), -4.0, 4.0)
    common = 0.5 * jnp.clip(jax.random.normal(shared_key, (1,) + shape[1:], jnp.float32), -4.0, 4.0)
    return scales * (noise + common)


def draw_sphere_map(key, part):
    key = jax.random.fold_in(key, 3)
    groups = PW_SUB // ROWS_DEV
    subs = PWAVES // PW_SUB
    keys = jax.random.split(key, groups)

    def one_group(group_key):
        return pick_distinct(group_key, COL_DEV * GRID, subs * ROWS_DEV)
    cells = jax.vmap(one_group)(keys)
    return cells.reshape(groups, subs, ROWS_DEV).transpose(1, 0, 2).reshape(subs, PW_SUB)


def draw_kinetic(key, part):
    key = jax.random.fold_in(key, 4)
    subs = PWAVES // PW_SUB
    ramp = 1.0 + 2.0 * jnp.arange(PWAVES, dtype=jnp.float32).reshape(subs, PW_SUB) / PWAVES
    base = jnp.exp(jax.random.uniform(key, (subs, PW_SUB), jnp.float32, math.log(0.1), math.log(10.0)))
    return base * ramp


def draw_form_factors(key, part):
    key = jax.random.fold_in(key, 6)
    subs = PWAVES // PW_SUB
    shape = (CHANNELS, subs, PW_SUB)
    ramp = 1.0 + 2.0 * jnp.arange(PW_SUB, dtype=jnp.float32) / PW_SUB
    base = jnp.clip(jax.random.normal(key, shape, jnp.float32), -4.0, 4.0)
    return base * ramp


def draw_column_map(key, part):
    key = jax.random.fold_in(key, 7)
    return pick_distinct(key, GRID * GRID, COLUMNS)


def touch_ends(result, key, smallest, high):
    spot = [jax.random.randint(jax.random.fold_in(key, axis), (), 0, length) for axis, length in enumerate(result.shape)]
    longest = result.shape.index(max(result.shape))
    neighbour = spot[:longest] + [(spot[longest] + 1) % result.shape[longest]] + spot[longest + 1:]
    return result.at[tuple(spot)].set(smallest).at[tuple(neighbour)].set(high)


def levels(key, dims, shards, smallest, high):
    loudness, own = 1.0, jax.random.fold_in(key, 6)
    for position, parts in shards:
        heights = jnp.exp(jax.random.uniform(jax.random.fold_in(own, position), (parts,), jnp.float32, smallest / len(shards), high / len(shards)))
        loudness = loudness * jnp.repeat(heights, dims[position] // parts).reshape([-1 if axis == position else 1 for axis in range(len(dims))])
    return loudness


def centred(rng, shape, scale, reach, cuts=(), kind=jnp.bfloat16):
    loudness = levels(rng, shape, cuts, -0.22, 0.18) if cuts else 1.0
    values = jax.random.normal(rng, shape, jnp.float32) * scale * loudness
    return jnp.minimum(jnp.maximum(values, -reach), reach).astype(kind)


def setup_inputs(seed: int = 0) -> dict:
    key_list = jax.random.split(jax.random.key(seed), 10)
    return {
        "basis_re": draw_basis_re(jax.random.fold_in(key_list[9], 71), 0),
        "basis_im": draw_basis_im(jax.random.fold_in(key_list[9], 71), 0),
        "potential": centred(key_list[2], (GRID, GRID, GRID), 3.0, 15.0, ((0, 16),), jnp.float32),
        "kinetic": draw_kinetic(jax.random.fold_in(key_list[9], 71), 0),
        "form_factors": draw_form_factors(jax.random.fold_in(key_list[9], 71), 0),
        "channel_strength": jnp.clip(jax.random.uniform(key_list[5], (CHANNELS,), jnp.float32, -4.0, 4.0), -4.0, 4.0),
        "sphere_map": draw_sphere_map(jax.random.fold_in(key_list[9], 71), 0),
        "column_map": draw_column_map(jax.random.fold_in(key_list[9], 71), 0),
        "atom_sites": touch_ends(jax.random.randint(key_list[8], (3, ATOMS), 0, GRID), jax.random.fold_in(key_list[8], 1), 0, GRID - 1).astype(jnp.int32),
    }


exact_mode = lax.Precision.HIGHEST

def contract(left, right, left_dim, right_dim):
    return lax.dot_general(left, right, (((left_dim,), (right_dim,)), ((), ())), precision=exact_mode, preferred_element_type=jnp.float32)

def conj_product(left_re, left_im, right_re, right_im, left_dim, scale):
    real = contract(left_re, right_re, left_dim, left_dim) + contract(left_im, right_im, left_dim, left_dim)
    imag = contract(left_re, right_im, left_dim, left_dim) - contract(left_im, right_re, left_dim, left_dim)
    return (real * scale, imag * scale)

def phase_table(depth, x_index, y_index, atom_sites, grid):
    turns = (depth[:, None] * atom_sites[0][None, :] + x_index[:, None] * atom_sites[1][None, :] + y_index[:, None] * atom_sites[2][None, :]) % grid
    angle = turns.astype(jnp.float32) * (2.0 * math.pi / grid)
    return jnp.concatenate([jnp.cos(angle).astype(jnp.bfloat16), jnp.sin(angle).astype(jnp.bfloat16)], 1)

def weigh(form, wave_re, wave_im):
    channels = form.shape[0]
    bands = wave_re.shape[0]
    part_re = (form[:, None, :] * wave_re[None]).reshape(channels * bands, -1)
    part_im = (form[:, None, :] * wave_im[None]).reshape(channels * bands, -1)
    return jnp.concatenate([part_re.astype(jnp.bfloat16), part_im.astype(jnp.bfloat16)], 0)

def project(weighted, phase):
    half = weighted.shape[0] // 2
    atoms = phase.shape[1] // 2
    mixed = jnp.dot(weighted, phase, preferred_element_type=jnp.float32)
    return (mixed[:half, :atoms] - mixed[half:, atoms:], mixed[:half, atoms:] + mixed[half:, :atoms])

def apply_back(form, sum_re, sum_im, strength, phase, root_waves):
    channels = form.shape[0]
    bands = sum_re.shape[0] // channels
    factor = jnp.repeat(strength, bands)[:, None]
    scaled_re = (factor * (sum_re / root_waves) / root_waves).astype(jnp.bfloat16)
    scaled_im = (factor * (sum_im / root_waves) / root_waves).astype(jnp.bfloat16)
    stacked = jnp.concatenate([jnp.concatenate([scaled_re, scaled_im], 1), jnp.concatenate([scaled_im, -scaled_re], 1)], 0)
    mixed = lax.dot_general(stacked, phase, (((1,), (1,)), ((), ())), preferred_element_type=jnp.float32)
    back_re = mixed[:channels * bands].reshape(channels, bands, -1)
    back_im = mixed[channels * bands:].reshape(channels, bands, -1)
    return (lax.optimization_barrier(jnp.sum(form[:, None, :] * back_re, 0)), lax.optimization_barrier(jnp.sum(form[:, None, :] * back_im, 0)))

def subtract_span(image_re, image_im, flat_re, flat_im, coef_re, coef_im):
    span_re = contract(coef_re, flat_re, 0, 0) - contract(coef_im, flat_im, 0, 0)
    span_im = contract(coef_re, flat_im, 0, 0) + contract(coef_im, flat_re, 0, 0)
    return (image_re - span_re, image_im - span_im)

def combine_rows(solved_re, solved_im, wave_re, wave_im):
    out_re = contract(solved_re, wave_re, 0, 0) - contract(solved_im, wave_im, 0, 0)
    out_im = contract(solved_re, wave_im, 0, 0) + contract(solved_im, wave_re, 0, 0)
    return (out_re, out_im)

def cholesky_upper(gram_re, gram_im):
    size = gram_re.shape[0]
    ticks = jnp.arange(size)

    def one_row(row_index, carry):
        upper_re, upper_im = carry
        column_re = upper_re[:, row_index]
        column_im = upper_im[:, row_index]
        total_re = gram_re[row_index] - (jnp.dot(column_re, upper_re, precision=exact_mode) + jnp.dot(column_im, upper_im, precision=exact_mode))
        total_im = gram_im[row_index] - (jnp.dot(column_re, upper_im, precision=exact_mode) - jnp.dot(column_im, upper_re, precision=exact_mode))
        pivot = jnp.sqrt(total_re[row_index])
        new_re = jnp.where(ticks >= row_index, total_re / pivot, 0.0)
        new_im = jnp.where(ticks > row_index, total_im / pivot, 0.0)
        return (upper_re.at[row_index].set(new_re), upper_im.at[row_index].set(new_im))
    zero = jnp.zeros((size, size), gram_re.dtype)
    return lax.fori_loop(0, size, one_row, (zero, zero))

def invert_upper(upper_re, upper_im):
    size = upper_re.shape[0]
    identity = jnp.eye(size, dtype=upper_re.dtype)

    def one_row(step_index, carry):
        solved_re, solved_im = carry
        row_index = size - 1 - step_index
        lead_re = upper_re[row_index]
        lead_im = upper_im[row_index]
        right_re = identity[row_index] - (jnp.dot(lead_re, solved_re, precision=exact_mode) - jnp.dot(lead_im, solved_im, precision=exact_mode))
        right_im = -(jnp.dot(lead_re, solved_im, precision=exact_mode) + jnp.dot(lead_im, solved_re, precision=exact_mode))
        pivot = upper_re[row_index, row_index]
        return (solved_re.at[row_index].set(right_re / pivot), solved_im.at[row_index].set(right_im / pivot))
    zero = jnp.zeros((size, size), upper_re.dtype)
    return lax.fori_loop(0, size, one_row, (zero, zero))

def reference(basis_re, basis_im, potential, kinetic, form_factors, channel_strength, sphere_map, column_map, atom_sites):
    block_of = jnp.arange(PW_SUB, dtype=jnp.int32) // ROWS_DEV
    depth = (sphere_map // COL_DEV).reshape(-1)
    column = (block_of[None, :] * COL_DEV + sphere_map % COL_DEV).reshape(-1)
    plane_pos = column_map[column]
    x_index = plane_pos // GRID
    y_index = plane_pos % GRID
    flat = (depth * GRID + x_index) * GRID + y_index
    psi_re = basis_re[BLOCKS - 1].reshape(SLAB, -1)
    psi_im = basis_im[BLOCKS - 1].reshape(SLAB, -1)

    def local_one(pair):
        wave_re, wave_im = pair
        empty = jnp.zeros((GRID * GRID * GRID,), jnp.float32)
        field = lax.complex(empty.at[flat].set(wave_re), empty.at[flat].set(wave_im)).reshape(GRID, GRID, GRID)
        spread = jnp.fft.ifftn(field)
        back = jnp.fft.fftn(potential * spread).reshape(-1)[flat]
        return (jnp.real(back), jnp.imag(back))
    local_re, local_im = lax.map(local_one, (psi_re, psi_im))
    form_flat = form_factors.reshape(CHANNELS, -1)
    weighted = weigh(form_flat, psi_re, psi_im)
    root_waves = math.sqrt(PWAVES)
    site_blocks = atom_sites.reshape(3, ATOMS // 64, 64).transpose(1, 0, 2)

    def one_block(carry, sites):
        phase = phase_table(depth, x_index, y_index, sites, GRID)
        sum_re, sum_im = project(weighted, phase)
        back_re, back_im = apply_back(form_flat, sum_re, sum_im, channel_strength, phase, root_waves)
        return ((carry[0] + back_re, carry[1] + back_im), None)
    zero = jnp.zeros((SLAB, PWAVES), jnp.float32)
    (near_re, near_im), unused = lax.scan(one_block, (zero, zero), site_blocks)
    kinetic_flat = kinetic.reshape(-1)
    image_re = kinetic_flat * psi_re + local_re + near_re
    image_im = kinetic_flat * psi_im + local_im + near_im
    flat_re = basis_re.reshape(BLOCKS * SLAB, -1)
    flat_im = basis_im.reshape(BLOCKS * SLAB, -1)
    coef_re, coef_im = conj_product(flat_re, flat_im, image_re, image_im, 1, 1.0 / PWAVES)
    res_re, res_im = subtract_span(image_re, image_im, flat_re, flat_im, coef_re, coef_im)
    gram_re, gram_im = conj_product(res_re, res_im, res_re, res_im, 1, 1.0 / PWAVES)
    upper_re, upper_im = cholesky_upper(gram_re, gram_im)
    solved_re, solved_im = invert_upper(upper_re, upper_im)
    next_re, next_im = combine_rows(solved_re, solved_im, res_re, res_im)
    return (next_re.reshape(SLAB, N_BAND, PW_SUB), next_im.reshape(SLAB, N_BAND, PW_SUB), coef_re.reshape(BLOCKS, SLAB, SLAB), coef_im.reshape(BLOCKS, SLAB, SLAB), upper_re, upper_im)
```

```python
import functools
import math

import jax
import jax.numpy as jnp
import numpy as np
from jax import lax
from jax.experimental import pallas as pl
from jax.experimental.pallas import tpu as pltpu
from jax.sharding import PartitionSpec as P

f32 = jnp.float32
bf16 = jnp.bfloat16
NN = (((1,), (0,)), ((), ()))
NT = (((1,), (1,)), ((), ()))
TN = (((0,), (0,)), ((), ()))


def dot(left, right, dims):
    return lax.dot_general(left, right, dims, preferred_element_type=f32)


def exact_dot(left, right, dims):
    return lax.dot_general(
        left, right, dims, precision=lax.Precision.HIGHEST, preferred_element_type=f32
    )


def halves(value):
    high = value.astype(bf16)
    return high, (value - high.astype(f32)).astype(bf16)


def dot_split(value, table_high, table_low, dims):
    high, low = halves(value)
    return (
        dot(high, table_high, dims) + dot(low, table_high, dims) + dot(high, table_low, dims)
    )


def table_halves(table):
    table = np.asarray(table, np.float32)
    high = table.astype(jnp.bfloat16)
    low = (table - high.astype(np.float32)).astype(jnp.bfloat16)
    return jnp.asarray(high), jnp.asarray(low)


def host_tables(grid, planes, wave_groups, span):
    ticks = np.arange(grid)
    angle = (ticks[:, None] * ticks[None, :] % grid) * (2.0 * math.pi / grid)
    cos, sin = np.cos(angle), np.sin(angle)
    lanes = wave_groups * span
    spread = np.zeros((2, grid, wave_groups, 2, span // 2))
    split_cos = cos.reshape(grid, wave_groups, planes)
    split_sin = sin.reshape(grid, wave_groups, planes)
    spread[0, :, :, 0, :planes] = split_cos
    spread[0, :, :, 1, :planes] = split_sin
    spread[1, :, :, 0, :planes] = -split_sin
    spread[1, :, :, 1, :planes] = split_cos
    spread = spread.reshape(2, grid, lanes)
    back = np.zeros((2, wave_groups, 2, span // 2, grid))
    scale = 1.0 / float(grid) ** 3
    rows_cos = cos.reshape(wave_groups, planes, grid) * scale
    rows_sin = sin.reshape(wave_groups, planes, grid) * scale
    back[0, :, 0, :planes] = rows_cos
    back[0, :, 1, :planes] = rows_sin
    back[1, :, 0, :planes] = -rows_sin
    back[1, :, 1, :planes] = rows_cos
    back = back.reshape(2, lanes, grid)
    return (
        *table_halves(spread),
        *table_halves(back),
        *table_halves(np.stack([cos, sin])),
    )


def cos_sin_192(turns, grid):
    quarter = grid // 4
    step = jnp.floor(turns * (1.0 / quarter) + 0.5)
    rest = turns - step * quarter
    x = rest * (2.0 * math.pi / grid)
    x2 = x * x
    sine = x + x * x2 * (
        -1.6666654611e-1 + x2 * (8.3321608736e-3 + x2 * -1.9515295891e-4)
    )
    cosine = (
        1.0
        - 0.5 * x2
        + x2 * x2 * (4.166664568298827e-2 + x2 * (-1.388731625493765e-3 + x2 * 2.443315711809948e-5))
    )
    count = step.astype(jnp.int32)
    odd = (count & 1) == 1
    flip_cos = ((count + 1) & 2) == 2
    flip_sin = (count & 2) == 2
    out_cos = jnp.where(odd, sine, cosine)
    out_sin = jnp.where(odd, cosine, sine)
    return (
        jnp.where(flip_cos, -out_cos, out_cos),
        jnp.where(flip_sin, -out_sin, out_sin),
    )


def kernel(
    cfg,
    pot_ref,
    basis_re_ref,
    basis_im_ref,
    kin_ref,
    form_ref,
    strength_ref,
    sphere_ref,
    cmap_ref,
    sites_ref,
    t1h_ref,
    t1l_ref,
    f2h_ref,
    f2l_ref,
    dh_ref,
    dl_ref,
    next_re_ref,
    next_im_ref,
    coef_re_ref,
    coef_im_ref,
    chol_re_ref,
    chol_im_ref,
    y1_buf,
    col_buf,
    col_s,
    ps_send,
    ps_recv,
    sc_send,
    sc_buf,
    out_s,
    out_send,
    out_buf,
    co_send,
    co_buf,
    gr_send,
    gr_buf,
    ct_s,
    phase_cos,
    phase_sin,
    send_sem,
    recv_sem,
):
    n_band, n_pw, slab, blocks, channels, planes, grid, col_dev, span, group = cfg
    n_dev = n_band * n_pw
    vectors = blocks * slab
    columns = n_pw * col_dev
    per_tile = 128 // span
    tiles = n_pw * span // 128
    atoms = sites_ref.shape[1]
    rows = 2 * slab * channels
    half_rows = slab * channels
    waves = kin_ref.shape[1]
    total_waves = n_dev * waves
    root_waves = math.sqrt(total_waves)
    s = lax.axis_index("band")
    q = lax.axis_index("pw")
    me = s * n_pw + q

    def coords(device):
        return (device // n_pw, lax.rem(device, n_pw))

    barrier = pltpu.get_barrier_semaphore()

    def greet(k, carry):
        device = lax.rem(me + k, n_dev)
        pl.semaphore_signal(
            barrier, inc=1, device_id=coords(device), device_id_type=pl.DeviceIdType.MESH
        )
        return carry

    lax.fori_loop(1, n_dev, greet, 0)

    def push(source, target, sem, limit=n_dev):
        def one(k, carry):
            device = lax.rem(me + k, n_dev)

            def go():
                pltpu.make_async_remote_copy(
                    src_ref=source(device),
                    dst_ref=target,
                    send_sem=send_sem.at[sem],
                    recv_sem=recv_sem.at[sem],
                    device_id=coords(device),
                    device_id_type=pl.DeviceIdType.MESH,
                ).start()

            if limit < n_dev:
                pl.when(device < limit)(go)
            else:
                go()
            return carry

        lax.fori_loop(1, n_dev, one, 0)

    def take(buf, sem, count):
        view = buf.at[pl.ds(0, count)]
        pltpu.make_async_copy(view, view, sem).wait()

    cells = sphere_ref[pl.ds(s, 1), :].astype(f32)
    depth = jnp.floor((cells + 0.5) * (1.0 / col_dev))
    column = cells - depth * col_dev
    mask = (
        lax.broadcasted_iota(jnp.int32, (col_dev, waves), 0) == column.astype(jnp.int32)
    ).astype(f32)
    one_hot = jnp.where(
        lax.broadcasted_iota(jnp.int32, (grid, waves), 0) == depth.astype(jnp.int32), 1.0, 0.0
    ).astype(bf16)
    flat_re = basis_re_ref[...]
    flat_im = basis_im_ref[...]
    psi_re = flat_re[vectors - slab :]
    psi_im = flat_im[vectors - slab :]
    placed = jnp.concatenate(
        [mask * psi_re[b : b + 1] for b in range(slab)]
        + [mask * psi_im[b : b + 1] for b in range(slab)],
        0,
    )
    high, low = halves(placed)
    field = dot(high, one_hot, NT) + dot(low, one_hot, NT)
    half = slab * col_dev
    spread = dot_split(field[:half], t1h_ref[0], t1l_ref[0], NN) + dot_split(
        field[half:], t1h_ref[1], t1l_ref[1], NN
    )
    for b in range(slab):
        for t in range(tiles):
            y1_buf[b, t] = spread[b * col_dev : (b + 1) * col_dev, t * 128 : (t + 1) * 128]

    pl.semaphore_wait(barrier, n_dev - 1)
    push(
        lambda device: y1_buf.at[device // n_pw, lax.rem(device, n_pw) // per_tile],
        col_buf.at[me],
        0,
    )
    col_buf[me] = y1_buf[s, q // per_tile]

    col_x = cmap_ref[...].astype(f32)
    all_x = jnp.floor((col_x + 0.5) * (1.0 / grid))
    all_y = col_x - all_x * grid
    own = lax.broadcasted_iota(jnp.int32, (col_dev, columns), 1) == (
        q * col_dev + lax.broadcasted_iota(jnp.int32, (col_dev, columns), 0)
    )
    own_x = jnp.sum(jnp.where(own, all_x, 0.0), 1, keepdims=True)
    own_y = jnp.sum(jnp.where(own, all_y, 0.0), 1, keepdims=True)
    wave_x = jnp.sum(mask * own_x, 0, keepdims=True)
    wave_y = jnp.sum(mask * own_y, 0, keepdims=True)
    places = jnp.concatenate([depth, wave_x, wave_y, jnp.zeros((5, waves), f32)], 0)
    sites = jnp.concatenate([sites_ref[...].astype(f32), jnp.zeros((5, atoms), f32)], 0)
    turns = dot(places.T.astype(bf16), sites.astype(bf16), NN)
    cosine, sine = cos_sin_192(turns, grid)
    phase_cos[...] = cosine.astype(bf16)
    phase_sin[...] = sine.astype(bf16)
    form = form_ref[:, pl.ds(s, 1), :].reshape(channels, waves)
    weighted = jnp.concatenate(
        [form * psi_re[b : b + 1] for b in range(slab)]
        + [form * psi_im[b : b + 1] for b in range(slab)],
        0,
    ).astype(bf16)
    with_cos = dot(weighted, phase_cos[...], NN)
    with_sin = dot(weighted, phase_sin[...], NN)
    sums = jnp.concatenate(
        [
            with_cos[:half_rows] - with_sin[half_rows:],
            with_sin[:half_rows] + with_cos[half_rows:],
        ],
        0,
    )
    parts = atoms // 128
    for t in range(parts):
        ps_send[:, t, :] = sums[:, t * 128 : (t + 1) * 128]
    push(lambda device: ps_send.at[device], ps_recv.at[me], 1, rows)

    def at_columns(position):
        ticks = lax.broadcasted_iota(jnp.int32, (grid, columns), 0)
        chosen = jnp.where(ticks == position.astype(jnp.int32), 1.0, 0.0).astype(bf16)
        return [dot(table[i], chosen, NN) for table in (dh_ref, dl_ref) for i in (0, 1)]

    xch, xsh, xcl, xsl = at_columns(all_x)
    x_cos = xch + xcl
    x_sin = xsh + xsl
    ych, ysh, ycl, ysl = [part.astype(bf16) for part in at_columns(all_y)]
    mre_high = jnp.concatenate([ych, -ysh], 1)
    mre_low = jnp.concatenate([ycl, -ysl], 1)
    mim_high = jnp.concatenate([ysh, ych], 1)
    mim_low = jnp.concatenate([ysl, ycl], 1)

    out_s[...] = jnp.zeros_like(out_s)
    base = lax.rem(q, per_tile) * span

    take(col_buf, recv_sem.at[0], n_dev - 1)
    gathered = col_buf[0:n_pw]
    for b in range(1, n_band):
        gathered = gathered + col_buf[b * n_pw : (b + 1) * n_pw]
    col_s[...] = gathered.reshape(columns, 128).T

    def own_row():
        ps_recv[me] = ps_send[me]
        take(ps_recv, recv_sem.at[1], n_dev - 1)
        total = jnp.sum(ps_recv[...], 0)
        strength = strength_ref[lax.rem(me, channels)]
        sc_send[...] = strength * (total * (1.0 / root_waves)) * (1.0 / root_waves)
        sc_buf[me] = sc_send[...]
        push(lambda device: sc_send, sc_buf.at[me], 2)

    if rows < n_dev:
        pl.when(me < rows)(own_row)
    else:
        own_row()

    def some_planes(step, carry):
        first = step * group
        mixed = []
        for i in range(group):
            part_re = col_s[pl.ds(base + first + i, 1), :]
            part_im = col_s[pl.ds(base + span // 2 + first + i, 1), :]
            mixed.append(
                jnp.concatenate(
                    [x_cos * part_re - x_sin * part_im, x_cos * part_im + x_sin * part_re], 1
                )
            )
        mixed = jnp.concatenate(mixed, 0)
        field_re = dot_split(mixed, mre_high, mre_low, NT)
        field_im = dot_split(mixed, mim_high, mim_low, NT)
        weight = pot_ref[pl.ds(first, group)].reshape(group * grid, grid)
        back = dot_split(field_re * weight, mre_high, mre_low, NN) + dot_split(
            field_im * weight, mim_high, mim_low, NN
        )
        for i in range(group):
            back_re = back[i * grid : (i + 1) * grid, :columns]
            back_im = back[i * grid : (i + 1) * grid, columns:]
            out_s[pl.ds(base + first + i, 1), :] = jnp.sum(
                x_cos * back_re + x_sin * back_im, 0, keepdims=True
            )
            out_s[pl.ds(base + span // 2 + first + i, 1), :] = jnp.sum(
                x_cos * back_im - x_sin * back_re, 0, keepdims=True
            )
        return carry

    lax.fori_loop(0, planes // group, some_planes, 0)
    out_send[...] = out_s[...].T.reshape(n_pw, col_dev, 128)
    push(lambda device: out_send.at[lax.rem(device, n_pw)], out_buf.at[me], 3)
    out_buf[me] = out_send[q]

    if rows < n_dev:
        pl.when(me < rows)(lambda: take(sc_buf, recv_sem.at[2], rows - 1))
        pl.when(me >= rows)(lambda: take(sc_buf, recv_sem.at[2], rows))
    else:
        take(sc_buf, recv_sem.at[2], rows - 1)
    scaled = jnp.concatenate([sc_buf[:, t, :] for t in range(parts)], 1)
    scaled_re = scaled[:half_rows]
    scaled_im = scaled[half_rows:]
    near = dot(
        jnp.concatenate([scaled_re, scaled_im], 0).astype(bf16), phase_cos[...], NT
    ) + dot(jnp.concatenate([scaled_im, -scaled_re], 0).astype(bf16), phase_sin[...], NT)
    near = [
        jnp.sum(form * near[i * channels : (i + 1) * channels], 0, keepdims=True)
        for i in range(2 * slab)
    ]
    psi_all = jnp.concatenate([psi_re, psi_im], 0)
    image = kin_ref[pl.ds(s, 1), :] * psi_all + jnp.concatenate(near, 0)

    take(out_buf, recv_sem.at[3], n_dev - 1)
    lines = []
    for b in range(slab):
        line = []
        for t in range(tiles):
            begin = b * n_pw + t * per_tile
            line.append(jnp.sum(out_buf[begin : begin + per_tile], 0))
        lines.append(jnp.concatenate(line, 1))
    lines = jnp.concatenate(lines, 0)
    high, low = halves(lines)
    depths = [
        dot(high, f2h_ref[i], NN) + dot(low, f2h_ref[i], NN) + dot(high, f2l_ref[i], NN)
        for i in (0, 1)
    ]
    high, low = halves(jnp.concatenate(depths, 0))
    read = dot(high, one_hot, NN) + dot(low, one_hot, NN)
    local = [
        jnp.sum(mask * read[i * col_dev : (i + 1) * col_dev], 0, keepdims=True)
        for i in range(2 * slab)
    ]
    image = image + jnp.concatenate(local, 0)

    def doubled(wave):
        first, second = wave[:slab], wave[slab:]
        return jnp.concatenate(
            [
                jnp.concatenate([first, second], 1),
                jnp.concatenate([second, -first], 1),
            ],
            0,
        )

    span_rows = jnp.concatenate([flat_re, flat_im], 0)
    span_double = jnp.concatenate(
        [jnp.concatenate([flat_re, flat_im], 1), jnp.concatenate([flat_im, -flat_re], 1)], 0
    )
    part = exact_dot(doubled(image), span_double, NT) * (1.0 / total_waves)
    co_send[...] = jnp.zeros_like(co_send)
    co_send[:, 0 : 2 * vectors] = part
    push(lambda device: co_send, co_buf.at[me], 4)
    co_buf[me] = co_send[...]
    take(co_buf, recv_sem.at[4], n_dev - 1)
    coef = jnp.sum(co_buf[...], 0)
    residue = image - exact_dot(coef[:, : 2 * vectors], span_rows, NN)

    residue_double = doubled(residue)
    part = exact_dot(residue_double, residue_double, NT) * (1.0 / total_waves)
    gr_send[...] = jnp.zeros_like(gr_send)
    gr_send[:, 0 : 2 * slab] = part
    push(lambda device: gr_send, gr_buf.at[me], 5)
    gr_buf[me] = gr_send[...]

    pad = -coef.shape[0] % 8
    tall = jnp.concatenate([coef, jnp.zeros((pad, coef.shape[1]), f32)], 0) if pad else coef
    ct_s[...] = tall.T
    for k in range(slab):
        line = ct_s[pl.ds(k, blocks, stride=slab), :]
        coef_re_ref[:, k, :] = line[:, :slab]
        coef_im_ref[:, k, :] = line[:, slab : 2 * slab]

    take(gr_buf, recv_sem.at[5], n_dev - 1)
    gram = jnp.sum(gr_buf[...], 0)

    lane = lax.broadcasted_iota(jnp.int32, (1, gram.shape[1]), 1)

    def entry(row, index):
        return jnp.sum(jnp.where(lane == index, row, 0.0), 1, keepdims=True)

    def moved(row):
        return pltpu.roll(row, gram.shape[1] - slab, 1)

    upper = []
    for r in range(slab):
        total_re = gram[r : r + 1]
        total_im = moved(gram[r : r + 1])
        for up_re, up_im in upper:
            a_re, a_im = entry(up_re, r), entry(up_im, r)
            total_re, total_im = (
                total_re - (a_re * up_re + a_im * up_im),
                total_im - (a_re * up_im - a_im * up_re),
            )
        pivot = jnp.sqrt(entry(total_re, r))
        ok = lane < slab
        upper.append(
            (
                jnp.where((lane >= r) & ok, total_re / pivot, 0.0),
                jnp.where((lane > r) & ok, total_im / pivot, 0.0),
            )
        )
    chol_re_ref[...] = jnp.concatenate([u[0] for u in upper], 0)[:, :slab]
    chol_im_ref[...] = jnp.concatenate([u[1] for u in upper], 0)[:, :slab]
    solved = []
    for e in range(slab):
        row_re = residue[e : e + 1]
        row_im = residue[slab + e : slab + e + 1]
        for b in range(e):
            r_re, r_im = entry(upper[b][0], e), entry(upper[b][1], e)
            row_re, row_im = (
                row_re - (solved[b][0] * r_re - solved[b][1] * r_im),
                row_im - (solved[b][0] * r_im + solved[b][1] * r_re),
            )
        inverse = 1.0 / entry(upper[e][0], e)
        solved.append((row_re * inverse, row_im * inverse))
    next_re_ref[...] = jnp.concatenate([x[0] for x in solved], 0)
    next_im_ref[...] = jnp.concatenate([x[1] for x in solved], 0)

    take(col_buf, send_sem.at[0], n_dev - 1)
    if rows < n_dev:
        pl.when(me < rows)(lambda: take(ps_recv, send_sem.at[1], rows - 1))
        pl.when(me >= rows)(lambda: take(ps_recv, send_sem.at[1], rows))
        pl.when(me < rows)(lambda: take(ps_recv, send_sem.at[2], n_dev - 1))
    else:
        take(ps_recv, send_sem.at[1], rows - 1)
        take(ps_recv, send_sem.at[2], n_dev - 1)
    take(out_buf, send_sem.at[3], n_dev - 1)
    take(co_buf, send_sem.at[4], n_dev - 1)
    take(gr_buf, send_sem.at[5], n_dev - 1)


def body(
    basis_re,
    basis_im,
    potential,
    kinetic,
    form_factors,
    channel_strength,
    sphere_map,
    column_map,
    atom_sites,
):
    blocks, slab, _, waves = basis_re.shape
    n_band = lax.axis_size("band")
    n_pw = lax.axis_size("pw")
    n_dev = n_band * n_pw
    planes, grid, _ = potential.shape
    channels = form_factors.shape[0]
    columns = column_map.shape[0]
    col_dev = columns // n_pw
    atoms = atom_sites.shape[1]
    vectors = blocks * slab
    rows = 2 * slab * channels
    span = 8
    while span < 2 * planes:
        span *= 2
    group = max(g for g in (1, 2, 3, 4) if planes % g == 0)
    tiles = n_pw * span // 128
    wide = -(-2 * vectors // 128) * 128
    assert slab == n_band and rows <= n_dev and n_pw * span % 128 == 0
    tables = host_tables(grid, planes, n_pw, span)
    cfg = (n_band, n_pw, slab, blocks, channels, planes, grid, col_dev, span, group)
    vmem = pl.BlockSpec(memory_space=pltpu.VMEM)
    smem = pl.BlockSpec(memory_space=pltpu.SMEM)
    parts = atoms // 128
    outs = pl.pallas_call(
        functools.partial(kernel, cfg),
        out_shape=[
            jax.ShapeDtypeStruct((slab, waves), f32),
            jax.ShapeDtypeStruct((slab, waves), f32),
            jax.ShapeDtypeStruct((blocks, slab, slab), f32),
            jax.ShapeDtypeStruct((blocks, slab, slab), f32),
            jax.ShapeDtypeStruct((slab, slab), f32),
            jax.ShapeDtypeStruct((slab, slab), f32),
        ],
        in_specs=[vmem] * 5 + [smem] + [vmem] * 9,
        out_specs=[vmem] * 6,
        scratch_shapes=[
            pltpu.VMEM((slab, tiles, col_dev, 128), f32),
            pltpu.VMEM((n_dev, col_dev, 128), f32),
            pltpu.VMEM((128, columns), f32),
            pltpu.VMEM((rows, parts, 128), f32),
            pltpu.VMEM((n_dev, parts, 128), f32),
            pltpu.VMEM((parts, 128), f32),
            pltpu.VMEM((rows, parts, 128), f32),
            pltpu.VMEM((128, columns), f32),
            pltpu.VMEM((n_pw, col_dev, 128), f32),
            pltpu.VMEM((n_dev, col_dev, 128), f32),
            pltpu.VMEM((2 * slab, wide), f32),
            pltpu.VMEM((n_dev, 2 * slab, wide), f32),
            pltpu.VMEM((2 * slab, 128), f32),
            pltpu.VMEM((n_dev, 2 * slab, 128), f32),
            pltpu.VMEM((wide, -(-2 * slab // 8) * 8), f32),
            pltpu.VMEM((waves, atoms), bf16),
            pltpu.VMEM((waves, atoms), bf16),
            pltpu.SemaphoreType.DMA((6,)),
            pltpu.SemaphoreType.DMA((6,)),
        ],
        compiler_params=pltpu.CompilerParams(
            collective_id=0, has_side_effects=True, vmem_limit_bytes=56 * 2**20
        ),
    )(
        potential,
        basis_re.reshape(vectors, waves),
        basis_im.reshape(vectors, waves),
        kinetic,
        form_factors,
        channel_strength,
        sphere_map,
        column_map.reshape(1, columns),
        atom_sites,
        *tables,
    )
    next_re, next_im, coef_re, coef_im, chol_re, chol_im = outs
    return (
        next_re.reshape(slab, 1, waves),
        next_im.reshape(slab, 1, waves),
        coef_re,
        coef_im,
        chol_re,
        chol_im,
    )


def solution(mesh):
    return jax.shard_map(
        body,
        mesh=mesh,
        in_specs=(
            P(None, None, "band", "pw"),
            P(None, None, "band", "pw"),
            P("pw", None, None),
            P(None, "pw"),
            P(None, None, "pw"),
            P(),
            P(None, "pw"),
            P(),
            P(),
        ),
        out_specs=(P(None, "band", "pw"), P(None, "band", "pw"), P(), P(), P(), P()),
        check_vma=False,
    )
```

```python
import functools
import math

import jax
import jax.numpy as jnp
import numpy as np
from jax import lax
from jax.experimental import pallas as pl
from jax.experimental.pallas import tpu as pltpu
from jax.sharding import PartitionSpec as P

f32 = jnp.float32
bf16 = jnp.bfloat16
NN = (((1,), (0,)), ((), ()))
NT = (((1,), (1,)), ((), ()))
TN = (((0,), (0,)), ((), ()))


def dot(left, right, dims):
    return lax.dot_general(left, right, dims, preferred_element_type=f32)


def exact_dot(left, right, dims):
    return lax.dot_general(
        left, right, dims, precision=lax.Precision.HIGHEST, preferred_element_type=f32
    )


def halves(value):
    high = value.astype(bf16)
    return high, (value - high.astype(f32)).astype(bf16)


def dot_split(value, table_high, table_low, dims):
    high, low = halves(value)
    return (
        dot(high, table_high, dims) + dot(low, table_high, dims) + dot(high, table_low, dims)
    )


def table_halves(table):
    table = np.asarray(table, np.float32)
    high = table.astype(jnp.bfloat16)
    low = (table - high.astype(np.float32)).astype(jnp.bfloat16)
    return jnp.asarray(high), jnp.asarray(low)


def host_tables(grid, planes, wave_groups, span):
    ticks = np.arange(grid)
    angle = (ticks[:, None] * ticks[None, :] % grid) * (2.0 * math.pi / grid)
    cos, sin = np.cos(angle), np.sin(angle)
    lanes = wave_groups * span
    spread = np.zeros((2, grid, wave_groups, 2, span // 2))
    split_cos = cos.reshape(grid, wave_groups, planes)
    split_sin = sin.reshape(grid, wave_groups, planes)
    spread[0, :, :, 0, :planes] = split_cos
    spread[0, :, :, 1, :planes] = split_sin
    spread[1, :, :, 0, :planes] = -split_sin
    spread[1, :, :, 1, :planes] = split_cos
    spread = spread.reshape(2, grid, lanes)
    back = np.zeros((2, wave_groups, 2, span // 2, grid))
    scale = 1.0 / float(grid) ** 3
    rows_cos = cos.reshape(wave_groups, planes, grid) * scale
    rows_sin = sin.reshape(wave_groups, planes, grid) * scale
    back[0, :, 0, :planes] = rows_cos
    back[0, :, 1, :planes] = rows_sin
    back[1, :, 0, :planes] = -rows_sin
    back[1, :, 1, :planes] = rows_cos
    back = back.reshape(2, lanes, grid)
    return (
        *table_halves(spread),
        *table_halves(back),
        *table_halves(np.stack([cos, sin])),
    )


def cos_sin_192(turns, grid):
    quarter = grid // 4
    step = jnp.floor(turns * (1.0 / quarter) + 0.5)
    rest = turns - step * quarter
    x = rest * (2.0 * math.pi / grid)
    x2 = x * x
    sine = x + x * x2 * (
        -1.6666654611e-1 + x2 * (8.3321608736e-3 + x2 * -1.9515295891e-4)
    )
    cosine = (
        1.0
        - 0.5 * x2
        + x2 * x2 * (4.166664568298827e-2 + x2 * (-1.388731625493765e-3 + x2 * 2.443315711809948e-5))
    )
    count = step.astype(jnp.int32)
    odd = (count & 1) == 1
    flip_cos = ((count + 1) & 2) == 2
    flip_sin = (count & 2) == 2
    out_cos = jnp.where(odd, sine, cosine)
    out_sin = jnp.where(odd, cosine, sine)
    return (
        jnp.where(flip_cos, -out_cos, out_cos),
        jnp.where(flip_sin, -out_sin, out_sin),
    )


def kernel(
    cfg,
    pot_ref,
    basis_re_ref,
    basis_im_ref,
    kin_ref,
    form_ref,
    strength_ref,
    sphere_ref,
    cmap_ref,
    sites_ref,
    t1h_ref,
    t1l_ref,
    f2h_ref,
    f2l_ref,
    dh_ref,
    dl_ref,
    packed_ref,
    y1_buf,
    col_buf,
    col_s,
    ps_send,
    ps_recv,
    sc_send,
    sc_buf,
    out_s,
    out_send,
    out_buf,
    co_send,
    co_buf,
    gr_send,
    gr_buf,
    phase_cos,
    phase_sin,
    pot_buf,
    f2h_buf,
    f2l_buf,
    dh_buf,
    dl_buf,
    send_sem,
    recv_sem,
    load_sem,
):
    n_band, n_pw, slab, blocks, channels, planes, grid, col_dev, span, group = cfg
    n_dev = n_band * n_pw
    vectors = blocks * slab
    columns = n_pw * col_dev
    per_tile = 128 // span
    tiles = n_pw * span // 128
    atoms = sites_ref.shape[1]
    rows = 2 * slab * channels
    half_rows = slab * channels
    waves = kin_ref.shape[1]
    total_waves = n_dev * waves
    root_waves = math.sqrt(total_waves)
    s = lax.axis_index("band")
    q = lax.axis_index("pw")
    me = s * n_pw + q

    def wrap(value, size):
        return jnp.where(value >= size, value - size, value)

    def others(act):
        for turn in range(n_band):
            band = wrap(s + turn, n_band)

            def one(k, carry):
                act(band, wrap(q + k, n_pw))
                return carry

            lax.fori_loop(1, n_pw, one, 0, unroll=n_dev <= 64)
            if turn:
                act(band, q)

    barrier = pltpu.get_barrier_semaphore()
    others(
        lambda band, pw: pl.semaphore_signal(
            barrier, inc=1, device_id=(band, pw), device_id_type=pl.DeviceIdType.MESH
        )
    )
    loads = [
        pltpu.make_async_copy(source, target, load_sem.at[i])
        for i, (source, target) in enumerate(
            [
                (dh_ref, dh_buf),
                (dl_ref, dl_buf),
                (pot_ref, pot_buf),
                (f2h_ref, f2h_buf),
                (f2l_ref, f2l_buf),
            ]
        )
    ]
    for load in loads:
        load.start()

    def push(source, target, sem, limit=n_dev):
        def one(band, pw):
            def go():
                pltpu.make_async_remote_copy(
                    src_ref=source(band, pw),
                    dst_ref=target,
                    send_sem=send_sem.at[sem],
                    recv_sem=recv_sem.at[sem],
                    device_id=(band, pw),
                    device_id_type=pl.DeviceIdType.MESH,
                ).start()

            if limit < n_dev:
                pl.when(band * n_pw + pw < limit)(go)
            else:
                go()

        others(one)

    def take(buf, sem, count):
        view = buf.at[pl.ds(0, count)]
        pltpu.make_async_copy(view, view, sem).wait()

    cells = sphere_ref[pl.ds(s, 1), :].astype(f32)
    depth = jnp.floor((cells + 0.5) * (1.0 / col_dev))
    column = cells - depth * col_dev
    mask = (
        lax.broadcasted_iota(jnp.int32, (col_dev, waves), 0) == column.astype(jnp.int32)
    ).astype(f32)
    one_hot = jnp.where(
        lax.broadcasted_iota(jnp.int32, (grid, waves), 0) == depth.astype(jnp.int32), 1.0, 0.0
    ).astype(bf16)
    flat_re, flat_im = [
        jnp.concatenate([ref[j, k] for j in range(blocks) for k in range(slab)], 0)
        for ref in (basis_re_ref, basis_im_ref)
    ]
    psi_re = flat_re[vectors - slab :]
    psi_im = flat_im[vectors - slab :]
    placed = jnp.concatenate(
        [mask * psi_re[b : b + 1] for b in range(slab)]
        + [mask * psi_im[b : b + 1] for b in range(slab)],
        0,
    )
    high, low = halves(placed)
    field = dot(high, one_hot, NT) + dot(low, one_hot, NT)
    half = slab * col_dev
    spread = dot_split(field[:half], t1h_ref[0], t1l_ref[0], NN) + dot_split(
        field[half:], t1h_ref[1], t1l_ref[1], NN
    )
    for b in range(slab):
        for t in range(tiles):
            y1_buf[b, t] = spread[b * col_dev : (b + 1) * col_dev, t * 128 : (t + 1) * 128]

    pl.semaphore_wait(barrier, n_dev - 1)
    push(
        lambda band, pw: y1_buf.at[band, pw // per_tile],
        col_buf.at[me],
        0,
    )
    col_buf[me] = y1_buf[s, q // per_tile]

    col_x = cmap_ref[...].astype(f32)
    all_x = jnp.floor((col_x + 0.5) * (1.0 / grid))
    all_y = col_x - all_x * grid
    own = lax.broadcasted_iota(jnp.int32, (col_dev, columns), 1) == (
        q * col_dev + lax.broadcasted_iota(jnp.int32, (col_dev, columns), 0)
    )
    own_x = jnp.sum(jnp.where(own, all_x, 0.0), 1, keepdims=True)
    own_y = jnp.sum(jnp.where(own, all_y, 0.0), 1, keepdims=True)
    wave_x = jnp.sum(mask * own_x, 0, keepdims=True)
    wave_y = jnp.sum(mask * own_y, 0, keepdims=True)
    places = jnp.concatenate([depth, wave_x, wave_y, jnp.zeros((5, waves), f32)], 0)
    sites = jnp.concatenate([sites_ref[...].astype(f32), jnp.zeros((5, atoms), f32)], 0)
    turns = dot(places.T.astype(bf16), sites.astype(bf16), NN)
    cosine, sine = cos_sin_192(turns, grid)
    phase_cos[...] = cosine.astype(bf16)
    phase_sin[...] = sine.astype(bf16)
    form = form_ref[:, pl.ds(s, 1), :].reshape(channels, waves)
    weighted = jnp.concatenate(
        [form * psi_re[b : b + 1] for b in range(slab)]
        + [form * psi_im[b : b + 1] for b in range(slab)],
        0,
    ).astype(bf16)
    with_cos = dot(weighted, phase_cos[...], NN)
    with_sin = dot(weighted, phase_sin[...], NN)
    sums = jnp.concatenate(
        [
            with_cos[:half_rows] - with_sin[half_rows:],
            with_sin[:half_rows] + with_cos[half_rows:],
        ],
        0,
    )
    parts = atoms // 128
    for t in range(parts):
        ps_send[:, t, :] = sums[:, t * 128 : (t + 1) * 128]
    push(lambda band, pw: ps_send.at[band * n_pw + pw], ps_recv.at[me], 1, rows)

    loads[0].wait()
    loads[1].wait()

    def at_columns(position):
        ticks = lax.broadcasted_iota(jnp.int32, (grid, columns), 0)
        chosen = jnp.where(ticks == position.astype(jnp.int32), 1.0, 0.0).astype(bf16)
        return [dot(table[i], chosen, NN) for table in (dh_buf, dl_buf) for i in (0, 1)]

    xch, xsh, xcl, xsl = at_columns(all_x)
    x_cos = xch + xcl
    x_sin = xsh + xsl
    ych, ysh, ycl, ysl = [part.astype(bf16) for part in at_columns(all_y)]
    mre_high = jnp.concatenate([ych, -ysh], 1)
    mre_low = jnp.concatenate([ycl, -ysl], 1)
    mim_high = jnp.concatenate([ysh, ych], 1)
    mim_low = jnp.concatenate([ysl, ycl], 1)

    out_s[...] = jnp.zeros_like(out_s)
    base = lax.rem(q, per_tile) * span

    take(col_buf, recv_sem.at[0], n_dev - 1)
    gathered = col_buf[0:n_pw]
    for b in range(1, n_band):
        gathered = gathered + col_buf[b * n_pw : (b + 1) * n_pw]
    col_s[...] = gathered.reshape(columns, 128).T

    def own_row():
        ps_recv[me] = ps_send[me]
        take(ps_recv, recv_sem.at[1], n_dev - 1)
        total = jnp.sum(ps_recv[...], 0)
        strength = strength_ref[lax.rem(me, channels)]
        sc_send[...] = strength * (total * (1.0 / root_waves)) * (1.0 / root_waves)
        sc_buf[me] = sc_send[...]
        push(lambda band, pw: sc_send, sc_buf.at[me], 2)

    if rows < n_dev:
        pl.when(me < rows)(own_row)
    else:
        own_row()

    loads[2].wait()

    def some_planes(step, carry):
        first = step * group
        mixed = []
        for i in range(group):
            part_re = col_s[pl.ds(base + first + i, 1), :]
            part_im = col_s[pl.ds(base + span // 2 + first + i, 1), :]
            mixed.append(
                jnp.concatenate(
                    [x_cos * part_re - x_sin * part_im, x_cos * part_im + x_sin * part_re], 1
                )
            )
        mixed = jnp.concatenate(mixed, 0)
        field_re = dot_split(mixed, mre_high, mre_low, NT)
        field_im = dot_split(mixed, mim_high, mim_low, NT)
        weight = pot_buf[pl.ds(first, group)].reshape(group * grid, grid)
        back = dot_split(field_re * weight, mre_high, mre_low, NN) + dot_split(
            field_im * weight, mim_high, mim_low, NN
        )
        for i in range(group):
            back_re = back[i * grid : (i + 1) * grid, :columns]
            back_im = back[i * grid : (i + 1) * grid, columns:]
            out_s[pl.ds(base + first + i, 1), :] = jnp.sum(
                x_cos * back_re + x_sin * back_im, 0, keepdims=True
            )
            out_s[pl.ds(base + span // 2 + first + i, 1), :] = jnp.sum(
                x_cos * back_im - x_sin * back_re, 0, keepdims=True
            )
        return carry

    lax.fori_loop(0, planes // group, some_planes, 0)
    out_send[...] = out_s[...].T.reshape(n_pw, col_dev, 128)
    push(lambda band, pw: out_send.at[pw], out_buf.at[me], 3)
    out_buf[me] = out_send[q]

    if rows < n_dev:
        pl.when(me < rows)(lambda: take(sc_buf, recv_sem.at[2], rows - 1))
        pl.when(me >= rows)(lambda: take(sc_buf, recv_sem.at[2], rows))
    else:
        take(sc_buf, recv_sem.at[2], rows - 1)
    scaled = jnp.concatenate([sc_buf[:, t, :] for t in range(parts)], 1)
    scaled_re = scaled[:half_rows]
    scaled_im = scaled[half_rows:]
    near = dot(
        jnp.concatenate([scaled_re, scaled_im], 0).astype(bf16), phase_cos[...], NT
    ) + dot(jnp.concatenate([scaled_im, -scaled_re], 0).astype(bf16), phase_sin[...], NT)
    near = [
        jnp.sum(form * near[i * channels : (i + 1) * channels], 0, keepdims=True)
        for i in range(2 * slab)
    ]
    psi_all = jnp.concatenate([psi_re, psi_im], 0)
    image = kin_ref[pl.ds(s, 1), :] * psi_all + jnp.concatenate(near, 0)

    loads[3].wait()
    loads[4].wait()
    take(out_buf, recv_sem.at[3], n_dev - 1)
    lines = []
    for b in range(slab):
        line = []
        for t in range(tiles):
            begin = b * n_pw + t * per_tile
            line.append(jnp.sum(out_buf[begin : begin + per_tile], 0))
        lines.append(jnp.concatenate(line, 1))
    lines = jnp.concatenate(lines, 0)
    high, low = halves(lines)
    depths = [
        dot(high, f2h_buf[i], NN) + dot(low, f2h_buf[i], NN) + dot(high, f2l_buf[i], NN)
        for i in (0, 1)
    ]
    high, low = halves(jnp.concatenate(depths, 0))
    read = dot(high, one_hot, NN) + dot(low, one_hot, NN)
    local = [
        jnp.sum(mask * read[i * col_dev : (i + 1) * col_dev], 0, keepdims=True)
        for i in range(2 * slab)
    ]
    image = image + jnp.concatenate(local, 0)

    def doubled(wave):
        first, second = wave[:slab], wave[slab:]
        return jnp.concatenate(
            [
                jnp.concatenate([first, second], 1),
                jnp.concatenate([second, -first], 1),
            ],
            0,
        )

    span_rows = jnp.concatenate([flat_re, flat_im], 0)
    span_double = jnp.concatenate(
        [jnp.concatenate([flat_re, flat_im], 1), jnp.concatenate([flat_im, -flat_re], 1)], 0
    )
    part = exact_dot(doubled(image), span_double, NT) * (1.0 / total_waves)
    co_send[...] = jnp.zeros_like(co_send)
    co_send[:, 0 : 2 * vectors] = part
    push(lambda band, pw: co_send, co_buf.at[me], 4)
    co_buf[me] = co_send[...]
    take(co_buf, recv_sem.at[4], n_dev - 1)
    coef = jnp.sum(co_buf[...], 0)
    residue = image - exact_dot(coef[:, : 2 * vectors], span_rows, NN)

    residue_double = doubled(residue)
    part = exact_dot(residue_double, residue_double, NT) * (1.0 / total_waves)
    gr_send[...] = jnp.zeros_like(gr_send)
    gr_send[:, 0 : 2 * slab] = part
    push(lambda band, pw: gr_send, gr_buf.at[me], 5)
    gr_buf[me] = gr_send[...]

    count = 2 * slab
    packed_ref[0:count] = residue
    packed_ref[count : 2 * count, 0 : coef.shape[1]] = coef

    take(gr_buf, recv_sem.at[5], n_dev - 1)
    packed_ref[2 * count : 3 * count, 0:128] = jnp.sum(gr_buf[...], 0)

    take(col_buf, send_sem.at[0], n_dev - 1)
    if rows < n_dev:
        pl.when(me < rows)(lambda: take(ps_recv, send_sem.at[1], rows - 1))
        pl.when(me >= rows)(lambda: take(ps_recv, send_sem.at[1], rows))
        pl.when(me < rows)(lambda: take(ps_recv, send_sem.at[2], n_dev - 1))
    else:
        take(ps_recv, send_sem.at[1], rows - 1)
        take(ps_recv, send_sem.at[2], n_dev - 1)
    take(out_buf, send_sem.at[3], n_dev - 1)
    take(co_buf, send_sem.at[4], n_dev - 1)
    take(gr_buf, send_sem.at[5], n_dev - 1)


def finish(
    slab,
    blocks,
    packed_ref,
    next_re_ref,
    next_im_ref,
    coef_re_ref,
    coef_im_ref,
    chol_re_ref,
    chol_im_ref,
):
    count = 2 * slab
    vectors = blocks * slab
    residue = packed_ref[0:count]
    gram = packed_ref[2 * count : 3 * count, 0:128]
    pick = (
        lax.broadcasted_iota(jnp.int32, (slab * blocks, vectors), 0),
        lax.broadcasted_iota(jnp.int32, (slab * blocks, vectors), 1),
    )
    order = (pick[1] == lax.rem(pick[0], blocks) * slab + pick[0] // blocks).astype(f32)
    for part, ref in ((0, coef_re_ref), (slab, coef_im_ref)):
        line = exact_dot(
            packed_ref[count + part : count + part + slab, 0:vectors], order, NT
        )
        for k in range(slab):
            ref[k] = line[:, k * blocks : (k + 1) * blocks]

    lane = lax.broadcasted_iota(jnp.int32, (1, gram.shape[1]), 1)

    def entry(row, index):
        return jnp.sum(jnp.where(lane == index, row, 0.0), 1, keepdims=True)

    def moved(row):
        return pltpu.roll(row, gram.shape[1] - slab, 1)

    upper = []
    for r in range(slab):
        total_re = gram[r : r + 1]
        total_im = moved(gram[r : r + 1])
        for up_re, up_im in upper:
            a_re, a_im = entry(up_re, r), entry(up_im, r)
            total_re, total_im = (
                total_re - (a_re * up_re + a_im * up_im),
                total_im - (a_re * up_im - a_im * up_re),
            )
        pivot = jnp.sqrt(entry(total_re, r))
        ok = lane < slab
        upper.append(
            (
                jnp.where((lane >= r) & ok, total_re / pivot, 0.0),
                jnp.where((lane > r) & ok, total_im / pivot, 0.0),
            )
        )
    chol_re_ref[...] = jnp.concatenate([u[0] for u in upper], 0)[:, :slab]
    chol_im_ref[...] = jnp.concatenate([u[1] for u in upper], 0)[:, :slab]
    solved = []
    for e in range(slab):
        row_re = residue[e : e + 1]
        row_im = residue[slab + e : slab + e + 1]
        for b in range(e):
            r_re, r_im = entry(upper[b][0], e), entry(upper[b][1], e)
            row_re, row_im = (
                row_re - (solved[b][0] * r_re - solved[b][1] * r_im),
                row_im - (solved[b][0] * r_im + solved[b][1] * r_re),
            )
        inverse = 1.0 / entry(upper[e][0], e)
        solved.append((row_re * inverse, row_im * inverse))
    for e in range(slab):
        next_re_ref[e] = solved[e][0]
        next_im_ref[e] = solved[e][1]


def body(
    basis_re,
    basis_im,
    potential,
    kinetic,
    form_factors,
    channel_strength,
    sphere_map,
    column_map,
    atom_sites,
):
    blocks, slab, _, waves = basis_re.shape
    n_band = lax.axis_size("band")
    n_pw = lax.axis_size("pw")
    n_dev = n_band * n_pw
    planes, grid, _ = potential.shape
    channels = form_factors.shape[0]
    columns = column_map.shape[0]
    col_dev = columns // n_pw
    atoms = atom_sites.shape[1]
    vectors = blocks * slab
    rows = 2 * slab * channels
    span = 8
    while span < 2 * planes:
        span *= 2
    group = max(g for g in (1, 2, 3, 4) if planes % g == 0)
    tiles = n_pw * span // 128
    wide = -(-2 * vectors // 128) * 128
    assert slab == n_band and rows <= n_dev and n_pw * span % 128 == 0
    tables = host_tables(grid, planes, n_pw, span)
    cfg = (n_band, n_pw, slab, blocks, channels, planes, grid, col_dev, span, group)
    vmem = pl.BlockSpec(memory_space=pltpu.VMEM)
    smem = pl.BlockSpec(memory_space=pltpu.SMEM)
    parts = atoms // 128
    anywhere = pl.BlockSpec(memory_space=pl.ANY)
    lanes = n_pw * span
    packed = pl.pallas_call(
        functools.partial(kernel, cfg),
        out_shape=jax.ShapeDtypeStruct((6 * slab, max(waves, wide)), f32),
        in_specs=[anywhere] + [vmem] * 4 + [smem] + [vmem] * 5 + [anywhere] * 4,
        out_specs=vmem,
        scratch_shapes=[
            pltpu.VMEM((slab, tiles, col_dev, 128), f32),
            pltpu.VMEM((n_dev, col_dev, 128), f32),
            pltpu.VMEM((128, columns), f32),
            pltpu.VMEM((rows, parts, 128), f32),
            pltpu.VMEM((n_dev, parts, 128), f32),
            pltpu.VMEM((parts, 128), f32),
            pltpu.VMEM((rows, parts, 128), f32),
            pltpu.VMEM((128, columns), f32),
            pltpu.VMEM((n_pw, col_dev, 128), f32),
            pltpu.VMEM((n_dev, col_dev, 128), f32),
            pltpu.VMEM((2 * slab, wide), f32),
            pltpu.VMEM((n_dev, 2 * slab, wide), f32),
            pltpu.VMEM((2 * slab, 128), f32),
            pltpu.VMEM((n_dev, 2 * slab, 128), f32),
            pltpu.VMEM((waves, atoms), bf16),
            pltpu.VMEM((waves, atoms), bf16),
            pltpu.VMEM((planes, grid, grid), f32),
            pltpu.VMEM((2, lanes, grid), bf16),
            pltpu.VMEM((2, lanes, grid), bf16),
            pltpu.VMEM((2, grid, grid), bf16),
            pltpu.VMEM((2, grid, grid), bf16),
            pltpu.SemaphoreType.DMA((6,)),
            pltpu.SemaphoreType.DMA((6,)),
            pltpu.SemaphoreType.DMA((5,)),
        ],
        compiler_params=pltpu.CompilerParams(
            collective_id=0, has_side_effects=True, vmem_limit_bytes=56 * 2**20
        ),
    )(
        potential,
        basis_re,
        basis_im,
        kinetic,
        form_factors,
        channel_strength,
        sphere_map,
        column_map.reshape(1, columns),
        atom_sites,
        *tables,
    )
    next_re, next_im, coef_re, coef_im, chol_re, chol_im = pl.pallas_call(
        functools.partial(finish, slab, blocks),
        out_shape=[
            jax.ShapeDtypeStruct((slab, 1, waves), f32),
            jax.ShapeDtypeStruct((slab, 1, waves), f32),
            jax.ShapeDtypeStruct((slab, slab, blocks), f32),
            jax.ShapeDtypeStruct((slab, slab, blocks), f32),
            jax.ShapeDtypeStruct((slab, slab), f32),
            jax.ShapeDtypeStruct((slab, slab), f32),
        ],
        in_specs=[vmem],
        out_specs=[vmem] * 6,
    )(packed)
    return (
        next_re,
        next_im,
        coef_re.transpose(2, 0, 1),
        coef_im.transpose(2, 0, 1),
        chol_re,
        chol_im,
    )


def solution(mesh):
    return jax.shard_map(
        body,
        mesh=mesh,
        in_specs=(
            P(None, None, "band", "pw"),
            P(None, None, "band", "pw"),
            P("pw", None, None),
            P(None, "pw"),
            P(None, None, "pw"),
            P(),
            P(None, "pw"),
            P(),
            P(),
        ),
        out_specs=(P(None, "band", "pw"), P(None, "band", "pw"), P(), P(), P(), P()),
        check_vma=False,
    )
```

```python
import functools
import math

import jax
import jax.numpy as jnp
import numpy as np
from jax import lax
from jax.experimental import pallas as pl
from jax.experimental.pallas import tpu as pltpu
from jax.sharding import PartitionSpec as P

f32 = jnp.float32
bf16 = jnp.bfloat16
NN = (((1,), (0,)), ((), ()))
NT = (((1,), (1,)), ((), ()))
TN = (((0,), (0,)), ((), ()))


def dot(left, right, dims):
    return lax.dot_general(left, right, dims, preferred_element_type=f32)


def exact_dot(left, right, dims):
    return lax.dot_general(
        left, right, dims, precision=lax.Precision.HIGHEST, preferred_element_type=f32
    )


def halves(value):
    high = value.astype(bf16)
    return high, (value - high.astype(f32)).astype(bf16)


def dot_split(value, table_high, table_low, dims):
    high, low = halves(value)
    return (
        dot(high, table_high, dims) + dot(low, table_high, dims) + dot(high, table_low, dims)
    )


def table_halves(table):
    table = np.asarray(table, np.float32)
    high = table.astype(jnp.bfloat16)
    low = (table - high.astype(np.float32)).astype(jnp.bfloat16)
    return jnp.asarray(high), jnp.asarray(low)


def host_tables(grid, planes, wave_groups, span):
    ticks = np.arange(grid)
    angle = (ticks[:, None] * ticks[None, :] % grid) * (2.0 * math.pi / grid)
    cos, sin = np.cos(angle), np.sin(angle)
    lanes = wave_groups * span
    spread = np.zeros((2, grid, wave_groups, 2, span // 2))
    split_cos = cos.reshape(grid, wave_groups, planes)
    split_sin = sin.reshape(grid, wave_groups, planes)
    spread[0, :, :, 0, :planes] = split_cos
    spread[0, :, :, 1, :planes] = split_sin
    spread[1, :, :, 0, :planes] = -split_sin
    spread[1, :, :, 1, :planes] = split_cos
    spread = spread.reshape(2, grid, lanes)
    back = np.zeros((2, wave_groups, 2, span // 2, grid))
    scale = 1.0 / float(grid) ** 3
    rows_cos = cos.reshape(wave_groups, planes, grid) * scale
    rows_sin = sin.reshape(wave_groups, planes, grid) * scale
    back[0, :, 0, :planes] = rows_cos
    back[0, :, 1, :planes] = rows_sin
    back[1, :, 0, :planes] = -rows_sin
    back[1, :, 1, :planes] = rows_cos
    back = back.reshape(2, lanes, grid)
    return (
        *table_halves(spread),
        *table_halves(back),
        *table_halves(np.stack([cos, sin])),
    )


def cos_sin_192(turns, grid):
    quarter = grid // 4
    step = jnp.floor(turns * (1.0 / quarter) + 0.5)
    rest = turns - step * quarter
    x = rest * (2.0 * math.pi / grid)
    x2 = x * x
    sine = x + x * x2 * (
        -1.6666654611e-1 + x2 * (8.3321608736e-3 + x2 * -1.9515295891e-4)
    )
    cosine = (
        1.0
        - 0.5 * x2
        + x2 * x2 * (4.166664568298827e-2 + x2 * (-1.388731625493765e-3 + x2 * 2.443315711809948e-5))
    )
    count = step.astype(jnp.int32)
    odd = (count & 1) == 1
    flip_cos = ((count + 1) & 2) == 2
    flip_sin = (count & 2) == 2
    out_cos = jnp.where(odd, sine, cosine)
    out_sin = jnp.where(odd, cosine, sine)
    return (
        jnp.where(flip_cos, -out_cos, out_cos),
        jnp.where(flip_sin, -out_sin, out_sin),
    )


def kernel(
    cfg,
    pot_ref,
    basis_re_ref,
    basis_im_ref,
    kin_ref,
    form_ref,
    strength_ref,
    sphere_ref,
    cmap_ref,
    sites_ref,
    t1h_ref,
    t1l_ref,
    f2h_ref,
    f2l_ref,
    dh_ref,
    dl_ref,
    packed_ref,
    y1_buf,
    col_buf,
    col_s,
    ps_send,
    ps_recv,
    sc_send,
    sc_buf,
    out_s,
    out_send,
    out_buf,
    row_pad,
    co_send,
    co_buf,
    gr_send,
    gr_buf,
    phase_cos,
    phase_sin,
    pot_buf,
    f2h_buf,
    f2l_buf,
    dh_buf,
    dl_buf,
    send_sem,
    recv_sem,
    load_sem,
):
    n_band, n_pw, slab, blocks, channels, planes, grid, col_dev, span, group = cfg
    n_dev = n_band * n_pw
    vectors = blocks * slab
    columns = n_pw * col_dev
    per_tile = 128 // span
    tiles = n_pw * span // 128
    fold_rows = col_dev // per_tile
    piece = fold_rows * n_pw
    atoms = sites_ref.shape[1]
    rows = 2 * slab * channels
    half_rows = slab * channels
    waves = kin_ref.shape[1]
    total_waves = n_dev * waves
    root_waves = math.sqrt(total_waves)
    s = lax.axis_index("band")
    q = lax.axis_index("pw")
    me = s * n_pw + q

    def wrap(value, size):
        return jnp.where(value >= size, value - size, value)

    def others(act):
        for turn in range(n_band):
            band = wrap(s + turn, n_band)

            def one(k, carry):
                act(band, wrap(q + k, n_pw))
                return carry

            lax.fori_loop(1, n_pw, one, 0, unroll=n_dev <= 64)
            if turn:
                act(band, q)

    barrier = pltpu.get_barrier_semaphore()
    others(
        lambda band, pw: pl.semaphore_signal(
            barrier, inc=1, device_id=(band, pw), device_id_type=pl.DeviceIdType.MESH
        )
    )
    loads = [
        pltpu.make_async_copy(source, target, load_sem.at[i])
        for i, (source, target) in enumerate(
            [
                (dh_ref, dh_buf),
                (dl_ref, dl_buf),
                (pot_ref, pot_buf),
                (f2h_ref, f2h_buf),
                (f2l_ref, f2l_buf),
            ]
        )
    ]
    for load in loads:
        load.start()

    def push(source, target, sem, limit=n_dev):
        def one(band, pw):
            def go():
                pltpu.make_async_remote_copy(
                    src_ref=source(band, pw),
                    dst_ref=target,
                    send_sem=send_sem.at[sem],
                    recv_sem=recv_sem.at[sem],
                    device_id=(band, pw),
                    device_id_type=pl.DeviceIdType.MESH,
                ).start()

            if limit < n_dev:
                pl.when(band * n_pw + pw < limit)(go)
            else:
                go()

        others(one)

    def take(buf, sem, count):
        view = buf.at[pl.ds(0, count)]
        pltpu.make_async_copy(view, view, sem).wait()

    cells = sphere_ref[pl.ds(s, 1), :].astype(f32)
    depth = jnp.floor((cells + 0.5) * (1.0 / col_dev))
    column = cells - depth * col_dev
    mask = (
        lax.broadcasted_iota(jnp.int32, (col_dev, waves), 0) == column.astype(jnp.int32)
    ).astype(f32)
    one_hot = jnp.where(
        lax.broadcasted_iota(jnp.int32, (grid, waves), 0) == depth.astype(jnp.int32), 1.0, 0.0
    ).astype(bf16)
    flat_re, flat_im = [
        jnp.concatenate([ref[j, k] for j in range(blocks) for k in range(slab)], 0)
        for ref in (basis_re_ref, basis_im_ref)
    ]
    psi_re = flat_re[vectors - slab :]
    psi_im = flat_im[vectors - slab :]
    placed = jnp.concatenate(
        [mask * psi_re[b : b + 1] for b in range(slab)]
        + [mask * psi_im[b : b + 1] for b in range(slab)],
        0,
    )
    high, low = halves(placed)
    field = dot(high, one_hot, NT) + dot(low, one_hot, NT)
    half = slab * col_dev
    spread = dot_split(field[:half], t1h_ref[0], t1l_ref[0], NN) + dot_split(
        field[half:], t1h_ref[1], t1l_ref[1], NN
    )
    block = lax.broadcasted_iota(jnp.int32, (col_dev, 128), 1) // span
    diagonal = lax.broadcasted_iota(jnp.int32, (col_dev, 128), 0) // fold_rows == block

    def turned(tile, turn):
        shift = turn % per_tile * span
        return pltpu.roll(tile, shift, 1) if shift else tile

    for b in range(slab):
        for t in range(tiles):
            tile = spread[b * col_dev : (b + 1) * col_dev, t * 128 : (t + 1) * 128]
            turns = [turned(tile, d) for d in range(per_tile)]
            for j in range(per_tile):
                message = turns[-j % per_tile]
                for g in range(1, per_tile):
                    message = jnp.where(block == g, turns[(g - j) % per_tile], message)
                message = jnp.where(diagonal, message, 0.0)
                shift = col_dev // 2
                while shift >= fold_rows:
                    message = message + pltpu.roll(message, shift, 0)
                    shift //= 2
                y1_buf[b, t * per_tile + j] = message[:fold_rows]

    pl.semaphore_wait(barrier, n_dev - 1)
    push(
        lambda band, pw: y1_buf.at[band, pw],
        col_buf.at[me],
        0,
    )
    col_buf[me] = y1_buf[s, q]

    col_x = cmap_ref[...].astype(f32)
    all_x = jnp.floor((col_x + 0.5) * (1.0 / grid))
    all_y = col_x - all_x * grid
    if columns <= 512:
        spot = lax.broadcasted_iota(jnp.int32, (columns, columns), 1)
        moved = lax.broadcasted_iota(jnp.int32, (columns, columns), 0) == (
            lax.rem(spot, n_pw) * col_dev + spot // n_pw
        )
        both = jnp.concatenate([all_x, all_y, jnp.zeros((6, columns), f32)], 0)
        both = dot(both.astype(bf16), jnp.where(moved, 1.0, 0.0).astype(bf16), NN)
        all_x, all_y = both[0:1], both[1:2]
    own = lax.broadcasted_iota(jnp.int32, (col_dev, columns), 1) == (
        lax.broadcasted_iota(jnp.int32, (col_dev, columns), 0) * n_pw + q
    )
    own_x = jnp.sum(jnp.where(own, all_x, 0.0), 1, keepdims=True)
    own_y = jnp.sum(jnp.where(own, all_y, 0.0), 1, keepdims=True)
    wave_x = jnp.sum(mask * own_x, 0, keepdims=True)
    wave_y = jnp.sum(mask * own_y, 0, keepdims=True)
    places = jnp.concatenate([depth, wave_x, wave_y, jnp.zeros((5, waves), f32)], 0)
    sites = jnp.concatenate([sites_ref[...].astype(f32), jnp.zeros((5, atoms), f32)], 0)
    turns = dot(places.T.astype(bf16), sites.astype(bf16), NN)
    cosine, sine = cos_sin_192(turns, grid)
    phase_cos[...] = cosine.astype(bf16)
    phase_sin[...] = sine.astype(bf16)
    form = form_ref[:, pl.ds(s, 1), :].reshape(channels, waves)
    weighted = jnp.concatenate(
        [form * psi_re[b : b + 1] for b in range(slab)]
        + [form * psi_im[b : b + 1] for b in range(slab)],
        0,
    ).astype(bf16)
    with_cos = dot(weighted, phase_cos[...], NN)
    with_sin = dot(weighted, phase_sin[...], NN)
    sums = jnp.concatenate(
        [
            with_cos[:half_rows] - with_sin[half_rows:],
            with_sin[:half_rows] + with_cos[half_rows:],
        ],
        0,
    )
    parts = atoms // 128
    for t in range(parts):
        ps_send[:, t, :] = sums[:, t * 128 : (t + 1) * 128]
    push(lambda band, pw: ps_send.at[band * n_pw + pw], ps_recv.at[me], 1, rows)

    loads[0].wait()
    loads[1].wait()

    def at_columns(position):
        ticks = lax.broadcasted_iota(jnp.int32, (grid, columns), 0)
        chosen = jnp.where(ticks == position.astype(jnp.int32), 1.0, 0.0).astype(bf16)
        return [dot(table[i], chosen, NN) for table in (dh_buf, dl_buf) for i in (0, 1)]

    xch, xsh, xcl, xsl = at_columns(all_x)
    x_cos = xch + xcl
    x_sin = xsh + xsl
    ych, ysh, ycl, ysl = [part.astype(bf16) for part in at_columns(all_y)]
    mre_high = jnp.concatenate([ych, -ysh], 1)
    mre_low = jnp.concatenate([ycl, -ysl], 1)
    mim_high = jnp.concatenate([ysh, ych], 1)
    mim_low = jnp.concatenate([ysl, ycl], 1)

    out_s[...] = jnp.zeros_like(out_s)

    take(col_buf, recv_sem.at[0], n_dev - 1)
    gathered = []
    for r in range(fold_rows):
        line = col_buf[:, r, :]
        total = line[0:n_pw]
        for b in range(1, n_band):
            total = total + line[b * n_pw : (b + 1) * n_pw]
        gathered.append(total)
    gathered = jnp.concatenate(gathered, 0).T
    col_s[...] = jnp.concatenate(
        [gathered[g * span : (g + 1) * span] for g in range(per_tile)], 1
    )

    def own_row():
        ps_recv[me] = ps_send[me]
        take(ps_recv, recv_sem.at[1], n_dev - 1)
        total = jnp.sum(ps_recv[...], 0)
        strength = strength_ref[lax.rem(me, channels)]
        sc_send[...] = strength * (total * (1.0 / root_waves)) * (1.0 / root_waves)
        sc_buf[me] = sc_send[...]
        push(lambda band, pw: sc_send, sc_buf.at[me], 2)

    if rows < n_dev:
        pl.when(me < rows)(own_row)
    else:
        own_row()

    loads[2].wait()

    def some_planes(step, carry):
        first = step * group
        mixed = []
        for i in range(group):
            part_re = col_s[pl.ds(first + i, 1), :]
            part_im = col_s[pl.ds(span // 2 + first + i, 1), :]
            mixed.append(
                jnp.concatenate(
                    [x_cos * part_re - x_sin * part_im, x_cos * part_im + x_sin * part_re], 1
                )
            )
        mixed = jnp.concatenate(mixed, 0)
        field_re = dot_split(mixed, mre_high, mre_low, NT)
        field_im = dot_split(mixed, mim_high, mim_low, NT)
        weight = pot_buf[pl.ds(first, group)].reshape(group * grid, grid)
        back = dot_split(field_re * weight, mre_high, mre_low, NN) + dot_split(
            field_im * weight, mim_high, mim_low, NN
        )
        for i in range(group):
            back_re = back[i * grid : (i + 1) * grid, :columns]
            back_im = back[i * grid : (i + 1) * grid, columns:]
            out_s[pl.ds(first + i, 1), :] = jnp.sum(
                x_cos * back_re + x_sin * back_im, 0, keepdims=True
            )
            out_s[pl.ds(span // 2 + first + i, 1), :] = jnp.sum(
                x_cos * back_im - x_sin * back_re, 0, keepdims=True
            )
        return carry

    lax.fori_loop(0, planes // group, some_planes, 0)
    flipped = out_s[...]
    flipped = jnp.concatenate(
        [flipped[:, g * piece : (g + 1) * piece] for g in range(per_tile)], 0
    ).T
    for r in range(fold_rows):
        out_send[:, r, :] = flipped[r * n_pw : (r + 1) * n_pw]
    push(lambda band, pw: out_send.at[pw], out_buf.at[me], 3)
    out_buf[me] = out_send[q]

    if rows < n_dev:
        pl.when(me < rows)(lambda: take(sc_buf, recv_sem.at[2], rows - 1))
        pl.when(me >= rows)(lambda: take(sc_buf, recv_sem.at[2], rows))
    else:
        take(sc_buf, recv_sem.at[2], rows - 1)
    scaled = jnp.concatenate([sc_buf[:, t, :] for t in range(parts)], 1)
    scaled_re = scaled[:half_rows]
    scaled_im = scaled[half_rows:]
    near = dot(
        jnp.concatenate([scaled_re, scaled_im], 0).astype(bf16), phase_cos[...], NT
    ) + dot(jnp.concatenate([scaled_im, -scaled_re], 0).astype(bf16), phase_sin[...], NT)
    near = [
        jnp.sum(form * near[i * channels : (i + 1) * channels], 0, keepdims=True)
        for i in range(2 * slab)
    ]
    psi_all = jnp.concatenate([psi_re, psi_im], 0)
    image = kin_ref[pl.ds(s, 1), :] * psi_all + jnp.concatenate(near, 0)

    loads[3].wait()
    loads[4].wait()
    take(out_buf, recv_sem.at[3], n_dev - 1)
    lines = []
    for b in range(slab):
        line = []
        for t in range(tiles):
            begin = b * n_pw + t * per_tile
            wide = [
                jnp.concatenate([out_buf[begin + j]] * per_tile, 0) for j in range(per_tile)
            ]
            tile = None
            for d in range(per_tile):
                part = wide[d]
                for g in range(1, per_tile):
                    part = jnp.where(block == g, wide[(g + d) % per_tile], part)
                part = turned(jnp.where(diagonal, part, 0.0), d)
                tile = part if tile is None else tile + part
            line.append(tile)
        lines.append(jnp.concatenate(line, 1))
    lines = jnp.concatenate(lines, 0)
    high, low = halves(lines)
    depths = [
        dot(high, f2h_buf[i], NN) + dot(low, f2h_buf[i], NN) + dot(high, f2l_buf[i], NN)
        for i in (0, 1)
    ]
    high, low = halves(jnp.concatenate(depths, 0))
    read = dot(high, one_hot, NN) + dot(low, one_hot, NN)
    local = [
        jnp.sum(mask * read[i * col_dev : (i + 1) * col_dev], 0, keepdims=True)
        for i in range(2 * slab)
    ]
    image = image + jnp.concatenate(local, 0)

    def doubled(wave):
        first, second = wave[:slab], wave[slab:]
        return jnp.concatenate(
            [
                jnp.concatenate([first, second], 1),
                jnp.concatenate([second, -first], 1),
            ],
            0,
        )

    span_rows = jnp.concatenate([flat_re, flat_im], 0)
    span_double = jnp.concatenate(
        [jnp.concatenate([flat_re, flat_im], 1), jnp.concatenate([flat_im, -flat_re], 1)], 0
    )
    count = 2 * slab
    wide = 2 * vectors
    folds = slab // co_send.shape[0]
    row_pad[...] = jnp.zeros_like(row_pad)
    row_pad[:, 0:wide] = exact_dot(doubled(image)[:slab], span_double, NT) * (
        1.0 / total_waves
    )
    for m in range(slab // folds):
        line = row_pad[m * folds : m * folds + 1, :]
        for i in range(1, folds):
            line = line + pltpu.roll(row_pad[m * folds + i : m * folds + i + 1, :], i * wide, 1)
        co_send[m : m + 1, :] = line
    push(lambda band, pw: co_send, co_buf.at[me], 4)
    co_buf[me] = co_send[...]
    take(co_buf, recv_sem.at[4], n_dev - 1)
    coef = jnp.sum(co_buf[...], 0)
    top = []
    for b in range(slab):
        line = coef[b // folds : b // folds + 1]
        if b % folds:
            line = pltpu.roll(line, 128 - b % folds * wide, 1)
        top.append(line[:, :wide])
    top = jnp.concatenate(top, 0)
    coef = jnp.concatenate(
        [top, jnp.concatenate([-top[:, vectors:], top[:, :vectors]], 1)], 0
    )
    residue = image - exact_dot(coef, span_rows, NN)

    residue_double = doubled(residue)
    row_pad[...] = jnp.zeros_like(row_pad)
    row_pad[:, 0:count] = exact_dot(residue_double[:slab], residue_double, NT) * (
        1.0 / total_waves
    )
    line = row_pad[0:1, :]
    for r in range(1, slab):
        line = line + pltpu.roll(row_pad[r : r + 1, :], r * count, 1)
    gr_send[...] = line
    push(lambda band, pw: gr_send, gr_buf.at[me], 5)
    gr_buf[me] = gr_send[...]

    packed_ref[0:count] = residue
    packed_ref[count : 2 * count, 0:wide] = coef
    take(gr_buf, recv_sem.at[5], n_dev - 1)
    gram = jnp.sum(gr_buf[...], 0)
    for r in range(slab):
        packed_ref[2 * count + r : 2 * count + r + 1, 0:128] = (
            pltpu.roll(gram, 128 - r * count, 1) if r else gram
        )

    take(col_buf, send_sem.at[0], n_dev - 1)
    if rows < n_dev:
        pl.when(me < rows)(lambda: take(ps_recv, send_sem.at[1], rows - 1))
        pl.when(me >= rows)(lambda: take(ps_recv, send_sem.at[1], rows))
        pl.when(me < rows)(lambda: take(ps_recv, send_sem.at[2], n_dev - 1))
    else:
        take(ps_recv, send_sem.at[1], rows - 1)
        take(ps_recv, send_sem.at[2], n_dev - 1)
    take(out_buf, send_sem.at[3], n_dev - 1)
    take(co_buf, send_sem.at[4], n_dev - 1)
    take(gr_buf, send_sem.at[5], n_dev - 1)


def finish(
    slab,
    blocks,
    packed_ref,
    next_re_ref,
    next_im_ref,
    coef_re_ref,
    coef_im_ref,
    chol_re_ref,
    chol_im_ref,
):
    count = 2 * slab
    vectors = blocks * slab
    residue = packed_ref[0:count]
    gram = packed_ref[2 * count : 3 * count, 0:128]
    pick = (
        lax.broadcasted_iota(jnp.int32, (slab * blocks, vectors), 0),
        lax.broadcasted_iota(jnp.int32, (slab * blocks, vectors), 1),
    )
    order = (pick[1] == lax.rem(pick[0], blocks) * slab + pick[0] // blocks).astype(f32)
    for part, ref in ((0, coef_re_ref), (slab, coef_im_ref)):
        line = exact_dot(
            packed_ref[count + part : count + part + slab, 0:vectors], order, NT
        )
        for k in range(slab):
            ref[k] = line[:, k * blocks : (k + 1) * blocks]

    lane = lax.broadcasted_iota(jnp.int32, (1, gram.shape[1]), 1)

    def entry(row, index):
        return jnp.sum(jnp.where(lane == index, row, 0.0), 1, keepdims=True)

    def moved(row):
        return pltpu.roll(row, gram.shape[1] - slab, 1)

    upper = []
    for r in range(slab):
        total_re = gram[r : r + 1]
        total_im = moved(gram[r : r + 1])
        for up_re, up_im in upper:
            a_re, a_im = entry(up_re, r), entry(up_im, r)
            total_re, total_im = (
                total_re - (a_re * up_re + a_im * up_im),
                total_im - (a_re * up_im - a_im * up_re),
            )
        pivot = jnp.sqrt(entry(total_re, r))
        ok = lane < slab
        upper.append(
            (
                jnp.where((lane >= r) & ok, total_re / pivot, 0.0),
                jnp.where((lane > r) & ok, total_im / pivot, 0.0),
            )
        )
    chol_re_ref[...] = jnp.concatenate([u[0] for u in upper], 0)[:, :slab]
    chol_im_ref[...] = jnp.concatenate([u[1] for u in upper], 0)[:, :slab]
    solved = []
    for e in range(slab):
        row_re = residue[e : e + 1]
        row_im = residue[slab + e : slab + e + 1]
        for b in range(e):
            r_re, r_im = entry(upper[b][0], e), entry(upper[b][1], e)
            row_re, row_im = (
                row_re - (solved[b][0] * r_re - solved[b][1] * r_im),
                row_im - (solved[b][0] * r_im + solved[b][1] * r_re),
            )
        inverse = 1.0 / entry(upper[e][0], e)
        solved.append((row_re * inverse, row_im * inverse))
    for e in range(slab):
        next_re_ref[e] = solved[e][0]
        next_im_ref[e] = solved[e][1]


def body(
    basis_re,
    basis_im,
    potential,
    kinetic,
    form_factors,
    channel_strength,
    sphere_map,
    column_map,
    atom_sites,
):
    blocks, slab, _, waves = basis_re.shape
    n_band = lax.axis_size("band")
    n_pw = lax.axis_size("pw")
    n_dev = n_band * n_pw
    planes, grid, _ = potential.shape
    channels = form_factors.shape[0]
    columns = column_map.shape[0]
    col_dev = columns // n_pw
    atoms = atom_sites.shape[1]
    vectors = blocks * slab
    rows = 2 * slab * channels
    span = 32
    while span < 2 * planes:
        span *= 2
    group = max(g for g in (1, 2, 3, 4) if planes % g == 0)
    lanes = n_pw * span
    fold_rows = col_dev * span // 128
    messages = max(1, slab * 2 * vectors // 128)
    assert slab == n_band and rows <= n_dev and lanes % 128 == 0
    assert span <= 128 and fold_rows * 128 == col_dev * span
    assert 2 * vectors <= 128 and 2 * slab * slab <= 128 and slab % messages == 0
    if columns > 512:
        column_map = column_map.reshape(n_pw, col_dev).T
    tables = host_tables(grid, planes, n_pw, span)
    cfg = (n_band, n_pw, slab, blocks, channels, planes, grid, col_dev, span, group)
    vmem = pl.BlockSpec(memory_space=pltpu.VMEM)
    smem = pl.BlockSpec(memory_space=pltpu.SMEM)
    parts = atoms // 128
    anywhere = pl.BlockSpec(memory_space=pl.ANY)
    packed = pl.pallas_call(
        functools.partial(kernel, cfg),
        out_shape=jax.ShapeDtypeStruct((6 * slab, max(waves, 128)), f32),
        in_specs=[anywhere] + [vmem] * 4 + [smem] + [vmem] * 5 + [anywhere] * 4,
        out_specs=vmem,
        scratch_shapes=[
            pltpu.VMEM((slab, n_pw, fold_rows, 128), f32),
            pltpu.VMEM((n_dev, fold_rows, 128), f32),
            pltpu.VMEM((span, columns), f32),
            pltpu.VMEM((rows, parts, 128), f32),
            pltpu.VMEM((n_dev, parts, 128), f32),
            pltpu.VMEM((parts, 128), f32),
            pltpu.VMEM((rows, parts, 128), f32),
            pltpu.VMEM((span, columns), f32),
            pltpu.VMEM((n_pw, fold_rows, 128), f32),
            pltpu.VMEM((n_dev, fold_rows, 128), f32),
            pltpu.VMEM((slab, 128), f32),
            pltpu.VMEM((messages, 128), f32),
            pltpu.VMEM((n_dev, messages, 128), f32),
            pltpu.VMEM((1, 128), f32),
            pltpu.VMEM((n_dev, 1, 128), f32),
            pltpu.VMEM((waves, atoms), bf16),
            pltpu.VMEM((waves, atoms), bf16),
            pltpu.VMEM((planes, grid, grid), f32),
            pltpu.VMEM((2, lanes, grid), bf16),
            pltpu.VMEM((2, lanes, grid), bf16),
            pltpu.VMEM((2, grid, grid), bf16),
            pltpu.VMEM((2, grid, grid), bf16),
            pltpu.SemaphoreType.DMA((6,)),
            pltpu.SemaphoreType.DMA((6,)),
            pltpu.SemaphoreType.DMA((5,)),
        ],
        compiler_params=pltpu.CompilerParams(
            collective_id=0, has_side_effects=True, vmem_limit_bytes=56 * 2**20
        ),
    )(
        potential,
        basis_re,
        basis_im,
        kinetic,
        form_factors,
        channel_strength,
        sphere_map,
        column_map.reshape(1, columns),
        atom_sites,
        *tables,
    )
    next_re, next_im, coef_re, coef_im, chol_re, chol_im = pl.pallas_call(
        functools.partial(finish, slab, blocks),
        out_shape=[
            jax.ShapeDtypeStruct((slab, 1, waves), f32),
            jax.ShapeDtypeStruct((slab, 1, waves), f32),
            jax.ShapeDtypeStruct((slab, slab, blocks), f32),
            jax.ShapeDtypeStruct((slab, slab, blocks), f32),
            jax.ShapeDtypeStruct((slab, slab), f32),
            jax.ShapeDtypeStruct((slab, slab), f32),
        ],
        in_specs=[vmem],
        out_specs=[vmem] * 6,
    )(packed)
    return (
        next_re,
        next_im,
        coef_re.transpose(2, 0, 1),
        coef_im.transpose(2, 0, 1),
        chol_re,
        chol_im,
    )


def solution(mesh):
    return jax.shard_map(
        body,
        mesh=mesh,
        in_specs=(
            P(None, None, "band", "pw"),
            P(None, None, "band", "pw"),
            P("pw", None, None),
            P(None, "pw"),
            P(None, None, "pw"),
            P(),
            P(None, "pw"),
            P(),
            P(),
        ),
        out_specs=(P(None, "band", "pw"), P(None, "band", "pw"), P(), P(), P(), P()),
        check_vma=False,
    )
```

```python
import functools
import math

import jax
import jax.numpy as jnp
import numpy as np
from jax import lax
from jax.experimental import pallas as pl
from jax.experimental.pallas import tpu as pltpu
from jax.sharding import PartitionSpec as P

f32 = jnp.float32
bf16 = jnp.bfloat16
NN = (((1,), (0,)), ((), ()))
NT = (((1,), (1,)), ((), ()))
TN = (((0,), (0,)), ((), ()))


def dot(left, right, dims):
    return lax.dot_general(left, right, dims, preferred_element_type=f32)


def exact_dot(left, right, dims):
    return lax.dot_general(
        left, right, dims, precision=lax.Precision.HIGHEST, preferred_element_type=f32
    )


def halves(value):
    high = value.astype(bf16)
    return high, (value - high.astype(f32)).astype(bf16)


def dot_split(value, table_high, table_low, dims):
    high, low = halves(value)
    return (
        dot(high, table_high, dims) + dot(low, table_high, dims) + dot(high, table_low, dims)
    )


def table_halves(table):
    table = np.asarray(table, np.float32)
    high = table.astype(jnp.bfloat16)
    low = (table - high.astype(np.float32)).astype(jnp.bfloat16)
    return jnp.asarray(high), jnp.asarray(low)


def host_tables(grid, planes, wave_groups, span):
    ticks = np.arange(grid)
    angle = (ticks[:, None] * ticks[None, :] % grid) * (2.0 * math.pi / grid)
    cos, sin = np.cos(angle), np.sin(angle)
    lanes = wave_groups * span
    spread = np.zeros((2, grid, wave_groups, 2, span // 2))
    split_cos = cos.reshape(grid, wave_groups, planes)
    split_sin = sin.reshape(grid, wave_groups, planes)
    spread[0, :, :, 0, :planes] = split_cos
    spread[0, :, :, 1, :planes] = split_sin
    spread[1, :, :, 0, :planes] = -split_sin
    spread[1, :, :, 1, :planes] = split_cos
    spread = spread.reshape(2, grid, lanes)
    back = np.zeros((2, wave_groups, 2, span // 2, grid))
    scale = 1.0 / float(grid) ** 3
    rows_cos = cos.reshape(wave_groups, planes, grid) * scale
    rows_sin = sin.reshape(wave_groups, planes, grid) * scale
    back[0, :, 0, :planes] = rows_cos
    back[0, :, 1, :planes] = rows_sin
    back[1, :, 0, :planes] = -rows_sin
    back[1, :, 1, :planes] = rows_cos
    back = back.reshape(2, lanes, grid)
    return (
        *table_halves(spread),
        *table_halves(back),
        *table_halves(np.stack([cos, sin])),
    )


def cos_sin_192(turns, grid):
    quarter = grid // 4
    step = jnp.floor(turns * (1.0 / quarter) + 0.5)
    rest = turns - step * quarter
    x = rest * (2.0 * math.pi / grid)
    x2 = x * x
    sine = x + x * x2 * (
        -1.6666654611e-1 + x2 * (8.3321608736e-3 + x2 * -1.9515295891e-4)
    )
    cosine = (
        1.0
        - 0.5 * x2
        + x2 * x2 * (4.166664568298827e-2 + x2 * (-1.388731625493765e-3 + x2 * 2.443315711809948e-5))
    )
    count = step.astype(jnp.int32)
    odd = (count & 1) == 1
    flip_cos = ((count + 1) & 2) == 2
    flip_sin = (count & 2) == 2
    out_cos = jnp.where(odd, sine, cosine)
    out_sin = jnp.where(odd, cosine, sine)
    return (
        jnp.where(flip_cos, -out_cos, out_cos),
        jnp.where(flip_sin, -out_sin, out_sin),
    )


def kernel(
    cfg,
    pot_ref,
    basis_re_ref,
    basis_im_ref,
    kin_ref,
    form_ref,
    strength_ref,
    sphere_ref,
    cmap_ref,
    sites_ref,
    t1h_ref,
    t1l_ref,
    f2h_ref,
    f2l_ref,
    dh_ref,
    dl_ref,
    packed_ref,
    y1_buf,
    col_buf,
    col_s,
    ps_send,
    ps_recv,
    sc_send,
    sc_buf,
    out_s,
    out_send,
    out_buf,
    row_pad,
    co_send,
    co_buf,
    gr_send,
    gr_buf,
    phase_cos,
    phase_sin,
    pot_buf,
    f2h_buf,
    f2l_buf,
    dh_buf,
    dl_buf,
    fwd_table,
    back_table,
    back_left,
    send_sem,
    recv_sem,
    load_sem,
):
    n_band, n_pw, slab, blocks, channels, planes, grid, col_dev, span, group = cfg
    n_dev = n_band * n_pw
    vectors = blocks * slab
    columns = n_pw * col_dev
    per_tile = 128 // span
    tiles = n_pw * span // 128
    fold_rows = col_dev // per_tile
    piece = fold_rows * n_pw
    atoms = sites_ref.shape[1]
    rows = 2 * slab * channels
    half_rows = slab * channels
    waves = kin_ref.shape[1]
    total_waves = n_dev * waves
    root_waves = math.sqrt(total_waves)
    s = lax.axis_index("band")
    q = lax.axis_index("pw")
    me = s * n_pw + q

    def wrap(value, size):
        return jnp.where(value >= size, value - size, value)

    def others(act):
        for turn in range(n_band):
            band = wrap(s + turn, n_band)

            def one(k, carry):
                act(band, wrap(q + k, n_pw))
                return carry

            lax.fori_loop(1, n_pw, one, 0, unroll=n_dev <= 64)
            if turn:
                act(band, q)

    barrier = pltpu.get_barrier_semaphore()
    others(
        lambda band, pw: pl.semaphore_signal(
            barrier, inc=1, device_id=(band, pw), device_id_type=pl.DeviceIdType.MESH
        )
    )
    loads = [
        pltpu.make_async_copy(source, target, load_sem.at[i])
        for i, (source, target) in enumerate(
            [
                (dh_ref, dh_buf),
                (dl_ref, dl_buf),
                (pot_ref, pot_buf),
                (f2h_ref, f2h_buf),
                (f2l_ref, f2l_buf),
            ]
        )
    ]
    for load in loads:
        load.start()

    def push(source, target, sem, limit=n_dev):
        def one(band, pw):
            def go():
                pltpu.make_async_remote_copy(
                    src_ref=source(band, pw),
                    dst_ref=target,
                    send_sem=send_sem.at[sem],
                    recv_sem=recv_sem.at[sem],
                    device_id=(band, pw),
                    device_id_type=pl.DeviceIdType.MESH,
                ).start()

            if limit < n_dev:
                pl.when(band * n_pw + pw < limit)(go)
            else:
                go()

        others(one)

    def take(buf, sem, count):
        view = buf.at[pl.ds(0, count)]
        pltpu.make_async_copy(view, view, sem).wait()

    cells = sphere_ref[pl.ds(s, 1), :].astype(f32)
    depth = jnp.floor((cells + 0.5) * (1.0 / col_dev))
    column = cells - depth * col_dev
    mask = (
        lax.broadcasted_iota(jnp.int32, (col_dev, waves), 0) == column.astype(jnp.int32)
    ).astype(f32)
    one_hot = jnp.where(
        lax.broadcasted_iota(jnp.int32, (grid, waves), 0) == depth.astype(jnp.int32), 1.0, 0.0
    ).astype(bf16)
    flat_re, flat_im = [
        jnp.concatenate([ref[j, k] for j in range(blocks) for k in range(slab)], 0)
        for ref in (basis_re_ref, basis_im_ref)
    ]
    psi_re = flat_re[vectors - slab :]
    psi_im = flat_im[vectors - slab :]
    placed = jnp.concatenate(
        [mask * psi_re[b : b + 1] for b in range(slab)]
        + [mask * psi_im[b : b + 1] for b in range(slab)],
        0,
    )
    high, low = halves(placed)
    field = dot(high, one_hot, NT) + dot(low, one_hot, NT)
    half = slab * col_dev
    spread = dot_split(field[:half], t1h_ref[0], t1l_ref[0], NN) + dot_split(
        field[half:], t1h_ref[1], t1l_ref[1], NN
    )
    block = lax.broadcasted_iota(jnp.int32, (col_dev, 128), 1) // span
    diagonal = lax.broadcasted_iota(jnp.int32, (col_dev, 128), 0) // fold_rows == block

    def turned(tile, turn):
        shift = turn % per_tile * span
        return pltpu.roll(tile, shift, 1) if shift else tile

    for b in range(slab):
        for t in range(tiles):
            tile = spread[b * col_dev : (b + 1) * col_dev, t * 128 : (t + 1) * 128]
            turns = [turned(tile, d) for d in range(per_tile)]
            for j in range(per_tile):
                message = turns[-j % per_tile]
                for g in range(1, per_tile):
                    message = jnp.where(block == g, turns[(g - j) % per_tile], message)
                message = jnp.where(diagonal, message, 0.0)
                shift = col_dev // 2
                while shift >= fold_rows:
                    message = message + pltpu.roll(message, shift, 0)
                    shift //= 2
                y1_buf[b, t * per_tile + j] = message[:fold_rows]

    pl.semaphore_wait(barrier, n_dev - 1)
    push(
        lambda band, pw: y1_buf.at[band, pw],
        col_buf.at[me],
        0,
    )
    col_buf[me] = y1_buf[s, q]

    col_x = cmap_ref[...].astype(f32)
    all_x = jnp.floor((col_x + 0.5) * (1.0 / grid))
    all_y = col_x - all_x * grid
    if columns <= 512:
        spot = lax.broadcasted_iota(jnp.int32, (columns, columns), 1)
        moved = lax.broadcasted_iota(jnp.int32, (columns, columns), 0) == (
            lax.rem(spot, n_pw) * col_dev + spot // n_pw
        )
        both = jnp.concatenate([all_x, all_y, jnp.zeros((6, columns), f32)], 0)
        both = dot(both.astype(bf16), jnp.where(moved, 1.0, 0.0).astype(bf16), NN)
        all_x, all_y = both[0:1], both[1:2]
    own = lax.broadcasted_iota(jnp.int32, (col_dev, columns), 1) == (
        lax.broadcasted_iota(jnp.int32, (col_dev, columns), 0) * n_pw + q
    )
    own_x = jnp.sum(jnp.where(own, all_x, 0.0), 1, keepdims=True)
    own_y = jnp.sum(jnp.where(own, all_y, 0.0), 1, keepdims=True)
    wave_x = jnp.sum(mask * own_x, 0, keepdims=True)
    wave_y = jnp.sum(mask * own_y, 0, keepdims=True)
    places = jnp.concatenate([depth, wave_x, wave_y, jnp.zeros((5, waves), f32)], 0)
    sites = jnp.concatenate([sites_ref[...].astype(f32), jnp.zeros((5, atoms), f32)], 0)
    turns = dot(places.T.astype(bf16), sites.astype(bf16), NN)
    cosine, sine = cos_sin_192(turns, grid)
    phase_cos[...] = cosine.astype(bf16)
    phase_sin[...] = sine.astype(bf16)
    form = form_ref[:, pl.ds(s, 1), :].reshape(channels, waves)
    weighted = jnp.concatenate(
        [form * psi_re[b : b + 1] for b in range(slab)]
        + [form * psi_im[b : b + 1] for b in range(slab)],
        0,
    ).astype(bf16)
    with_cos = dot(weighted, phase_cos[...], NN)
    with_sin = dot(weighted, phase_sin[...], NN)
    sums = jnp.concatenate(
        [
            with_cos[:half_rows] - with_sin[half_rows:],
            with_sin[:half_rows] + with_cos[half_rows:],
        ],
        0,
    )
    parts = atoms // 128
    for t in range(parts):
        ps_send[:, t, :] = sums[:, t * 128 : (t + 1) * 128]
    push(lambda band, pw: ps_send.at[band * n_pw + pw], ps_recv.at[me], 1, rows)

    loads[0].wait()
    loads[1].wait()

    def at_columns(position):
        ticks = lax.broadcasted_iota(jnp.int32, (grid, columns), 0)
        chosen = jnp.where(ticks == position.astype(jnp.int32), 1.0, 0.0).astype(bf16)
        return [dot(table[i], chosen, NN) for table in (dh_buf, dl_buf) for i in (0, 1)]

    xch, xsh, xcl, xsl = at_columns(all_x)
    x_cos = xch + xcl
    x_sin = xsh + xsl
    ych, ysh, ycl, ysl = [part.astype(bf16) for part in at_columns(all_y)]
    joined = columns <= 512
    mre_high = jnp.concatenate([ych, -ysh], 1)
    mre_low = jnp.concatenate([ycl, -ysl], 1)
    mim_high = jnp.concatenate([ysh, ych], 1)
    mim_low = jnp.concatenate([ysl, ycl], 1)

    if joined:
        gap = jnp.zeros((256 - grid, 2 * columns), bf16)
        high = jnp.concatenate([mre_high, gap, mim_high, gap], 0)
        low = jnp.concatenate([mre_low, gap, mim_low, gap], 0)
        fwd_table[...] = jnp.concatenate([high, high, low], 1)
        back_table[...] = jnp.concatenate(
            [mre_high, gap, mre_high, gap, mim_high, gap, mim_high, gap, low], 0
        )
        back_left[...] = jnp.zeros_like(back_left)
    out_s[...] = jnp.zeros_like(out_s)

    take(col_buf, recv_sem.at[0], n_dev - 1)
    gathered = []
    for r in range(fold_rows):
        line = col_buf[:, r, :]
        total = line[0:n_pw]
        for b in range(1, n_band):
            total = total + line[b * n_pw : (b + 1) * n_pw]
        gathered.append(total)
    gathered = jnp.concatenate(gathered, 0).T
    col_s[...] = jnp.concatenate(
        [gathered[g * span : (g + 1) * span] for g in range(per_tile)], 1
    )

    loads[2].wait()

    def some_planes(step, carry):
        first = step * group
        mixed = []
        for i in range(group):
            part_re = col_s[pl.ds(first + i, 1), :]
            part_im = col_s[pl.ds(span // 2 + first + i, 1), :]
            mixed.append(
                jnp.concatenate(
                    [x_cos * part_re - x_sin * part_im, x_cos * part_im + x_sin * part_re], 1
                )
            )
        mixed = jnp.concatenate(mixed, 0)
        weight = pot_buf[pl.ds(first, group)].reshape(group * grid, grid)
        if joined:
            high, low = halves(mixed)
            field = dot(jnp.concatenate([high, low, high], 1), fwd_table[...], NT)
            re_high, re_low = halves(field[:, :grid] * weight)
            im_high, im_low = halves(field[:, 256 : 256 + grid] * weight)
            for i, part in enumerate((re_low, re_high, im_high, im_low)):
                back_left[:, i * 256 : i * 256 + grid] = part
            back = dot(back_left[...], back_table[0:1024], NN) + dot(
                back_left[:, 256:768], back_table[1024:1536], NN
            )
        else:
            field_re = dot_split(mixed, mre_high, mre_low, NT)
            field_im = dot_split(mixed, mim_high, mim_low, NT)
            back = dot_split(field_re * weight, mre_high, mre_low, NN) + dot_split(
                field_im * weight, mim_high, mim_low, NN
            )
        for i in range(group):
            back_re = back[i * grid : (i + 1) * grid, :columns]
            back_im = back[i * grid : (i + 1) * grid, columns:]
            out_s[pl.ds(first + i, 1), :] = jnp.sum(
                x_cos * back_re + x_sin * back_im, 0, keepdims=True
            )
            out_s[pl.ds(span // 2 + first + i, 1), :] = jnp.sum(
                x_cos * back_im - x_sin * back_re, 0, keepdims=True
            )
        return carry

    some_planes(0, 0)

    def own_row():
        ps_recv[me] = ps_send[me]
        take(ps_recv, recv_sem.at[1], n_dev - 1)
        total = jnp.sum(ps_recv[...], 0)
        strength = strength_ref[lax.rem(me, channels)]
        sc_send[...] = strength * (total * (1.0 / root_waves)) * (1.0 / root_waves)
        sc_buf[me] = sc_send[...]
        push(lambda band, pw: sc_send, sc_buf.at[me], 2)

    if rows < n_dev:
        pl.when(me < rows)(own_row)
    else:
        own_row()

    if planes > group:
        lax.fori_loop(1, planes // group, some_planes, 0)
    flipped = out_s[...]
    flipped = jnp.concatenate(
        [flipped[:, g * piece : (g + 1) * piece] for g in range(per_tile)], 0
    ).T
    for r in range(fold_rows):
        out_send[:, r, :] = flipped[r * n_pw : (r + 1) * n_pw]
    push(lambda band, pw: out_send.at[pw], out_buf.at[me], 3)
    out_buf[me] = out_send[q]

    if rows < n_dev:
        pl.when(me < rows)(lambda: take(sc_buf, recv_sem.at[2], rows - 1))
        pl.when(me >= rows)(lambda: take(sc_buf, recv_sem.at[2], rows))
    else:
        take(sc_buf, recv_sem.at[2], rows - 1)
    scaled = jnp.concatenate([sc_buf[:, t, :] for t in range(parts)], 1)
    scaled_re = scaled[:half_rows]
    scaled_im = scaled[half_rows:]
    near = dot(
        jnp.concatenate([scaled_re, scaled_im], 0).astype(bf16), phase_cos[...], NT
    ) + dot(jnp.concatenate([scaled_im, -scaled_re], 0).astype(bf16), phase_sin[...], NT)
    near = [
        jnp.sum(form * near[i * channels : (i + 1) * channels], 0, keepdims=True)
        for i in range(2 * slab)
    ]
    psi_all = jnp.concatenate([psi_re, psi_im], 0)
    image = kin_ref[pl.ds(s, 1), :] * psi_all + jnp.concatenate(near, 0)

    loads[3].wait()
    loads[4].wait()
    take(out_buf, recv_sem.at[3], n_dev - 1)
    lines = []
    for b in range(slab):
        line = []
        for t in range(tiles):
            begin = b * n_pw + t * per_tile
            wide = [
                jnp.concatenate([out_buf[begin + j]] * per_tile, 0) for j in range(per_tile)
            ]
            tile = None
            for d in range(per_tile):
                part = wide[d]
                for g in range(1, per_tile):
                    part = jnp.where(block == g, wide[(g + d) % per_tile], part)
                part = turned(jnp.where(diagonal, part, 0.0), d)
                tile = part if tile is None else tile + part
            line.append(tile)
        lines.append(jnp.concatenate(line, 1))
    lines = jnp.concatenate(lines, 0)
    high, low = halves(lines)
    depths = [
        dot(high, f2h_buf[i], NN) + dot(low, f2h_buf[i], NN) + dot(high, f2l_buf[i], NN)
        for i in (0, 1)
    ]
    high, low = halves(jnp.concatenate(depths, 0))
    read = dot(high, one_hot, NN) + dot(low, one_hot, NN)
    local = [
        jnp.sum(mask * read[i * col_dev : (i + 1) * col_dev], 0, keepdims=True)
        for i in range(2 * slab)
    ]
    image = image + jnp.concatenate(local, 0)

    def doubled(wave):
        first, second = wave[:slab], wave[slab:]
        return jnp.concatenate(
            [
                jnp.concatenate([first, second], 1),
                jnp.concatenate([second, -first], 1),
            ],
            0,
        )

    span_rows = jnp.concatenate([flat_re, flat_im], 0)
    span_double = jnp.concatenate(
        [jnp.concatenate([flat_re, flat_im], 1), jnp.concatenate([flat_im, -flat_re], 1)], 0
    )
    count = 2 * slab
    wide = 2 * vectors
    folds = slab // co_send.shape[0]
    row_pad[...] = jnp.zeros_like(row_pad)
    row_pad[:, 0:wide] = exact_dot(doubled(image)[:slab], span_double, NT) * (
        1.0 / total_waves
    )
    for m in range(slab // folds):
        line = row_pad[m * folds : m * folds + 1, :]
        for i in range(1, folds):
            line = line + pltpu.roll(row_pad[m * folds + i : m * folds + i + 1, :], i * wide, 1)
        co_send[m : m + 1, :] = line
    push(lambda band, pw: co_send, co_buf.at[me], 4)
    co_buf[me] = co_send[...]
    take(co_buf, recv_sem.at[4], n_dev - 1)
    coef = jnp.sum(co_buf[...], 0)
    top = []
    for b in range(slab):
        line = coef[b // folds : b // folds + 1]
        if b % folds:
            line = pltpu.roll(line, 128 - b % folds * wide, 1)
        top.append(line[:, :wide])
    top = jnp.concatenate(top, 0)
    coef = jnp.concatenate(
        [top, jnp.concatenate([-top[:, vectors:], top[:, :vectors]], 1)], 0
    )
    residue = image - exact_dot(coef, span_rows, NN)

    residue_double = doubled(residue)
    row_pad[...] = jnp.zeros_like(row_pad)
    row_pad[:, 0:count] = exact_dot(residue_double[:slab], residue_double, NT) * (
        1.0 / total_waves
    )
    line = row_pad[0:1, :]
    for r in range(1, slab):
        line = line + pltpu.roll(row_pad[r : r + 1, :], r * count, 1)
    gr_send[...] = line
    push(lambda band, pw: gr_send, gr_buf.at[me], 5)
    gr_buf[me] = gr_send[...]

    packed_ref[0:count] = residue
    packed_ref[count : 2 * count, 0:wide] = coef
    take(gr_buf, recv_sem.at[5], n_dev - 1)
    gram = jnp.sum(gr_buf[...], 0)
    for r in range(slab):
        packed_ref[2 * count + r : 2 * count + r + 1, 0:128] = (
            pltpu.roll(gram, 128 - r * count, 1) if r else gram
        )

    take(col_buf, send_sem.at[0], n_dev - 1)
    if rows < n_dev:
        pl.when(me < rows)(lambda: take(ps_recv, send_sem.at[1], rows - 1))
        pl.when(me >= rows)(lambda: take(ps_recv, send_sem.at[1], rows))
        pl.when(me < rows)(lambda: take(ps_recv, send_sem.at[2], n_dev - 1))
    else:
        take(ps_recv, send_sem.at[1], rows - 1)
        take(ps_recv, send_sem.at[2], n_dev - 1)
    take(out_buf, send_sem.at[3], n_dev - 1)
    take(co_buf, send_sem.at[4], n_dev - 1)
    take(gr_buf, send_sem.at[5], n_dev - 1)


def finish(
    slab,
    blocks,
    packed_ref,
    next_re_ref,
    next_im_ref,
    coef_re_ref,
    coef_im_ref,
    chol_re_ref,
    chol_im_ref,
):
    count = 2 * slab
    vectors = blocks * slab
    residue = packed_ref[0:count]
    gram = packed_ref[2 * count : 3 * count, 0:128]
    pick = (
        lax.broadcasted_iota(jnp.int32, (slab * blocks, vectors), 0),
        lax.broadcasted_iota(jnp.int32, (slab * blocks, vectors), 1),
    )
    order = (pick[1] == lax.rem(pick[0], blocks) * slab + pick[0] // blocks).astype(f32)
    for part, ref in ((0, coef_re_ref), (slab, coef_im_ref)):
        line = exact_dot(
            packed_ref[count + part : count + part + slab, 0:vectors], order, NT
        )
        for k in range(slab):
            ref[k] = line[:, k * blocks : (k + 1) * blocks]

    lane = lax.broadcasted_iota(jnp.int32, (1, gram.shape[1]), 1)

    def entry(row, index):
        return jnp.sum(jnp.where(lane == index, row, 0.0), 1, keepdims=True)

    def moved(row):
        return pltpu.roll(row, gram.shape[1] - slab, 1)

    upper = []
    for r in range(slab):
        total_re = gram[r : r + 1]
        total_im = moved(gram[r : r + 1])
        for up_re, up_im in upper:
            a_re, a_im = entry(up_re, r), entry(up_im, r)
            total_re, total_im = (
                total_re - (a_re * up_re + a_im * up_im),
                total_im - (a_re * up_im - a_im * up_re),
            )
        pivot = jnp.sqrt(entry(total_re, r))
        ok = lane < slab
        upper.append(
            (
                jnp.where((lane >= r) & ok, total_re / pivot, 0.0),
                jnp.where((lane > r) & ok, total_im / pivot, 0.0),
            )
        )
    chol_re_ref[...] = jnp.concatenate([u[0] for u in upper], 0)[:, :slab]
    chol_im_ref[...] = jnp.concatenate([u[1] for u in upper], 0)[:, :slab]
    solved = []
    for e in range(slab):
        row_re = residue[e : e + 1]
        row_im = residue[slab + e : slab + e + 1]
        for b in range(e):
            r_re, r_im = entry(upper[b][0], e), entry(upper[b][1], e)
            row_re, row_im = (
                row_re - (solved[b][0] * r_re - solved[b][1] * r_im),
                row_im - (solved[b][0] * r_im + solved[b][1] * r_re),
            )
        inverse = 1.0 / entry(upper[e][0], e)
        solved.append((row_re * inverse, row_im * inverse))
    for e in range(slab):
        next_re_ref[e] = solved[e][0]
        next_im_ref[e] = solved[e][1]


def body(
    basis_re,
    basis_im,
    potential,
    kinetic,
    form_factors,
    channel_strength,
    sphere_map,
    column_map,
    atom_sites,
):
    blocks, slab, _, waves = basis_re.shape
    n_band = lax.axis_size("band")
    n_pw = lax.axis_size("pw")
    n_dev = n_band * n_pw
    planes, grid, _ = potential.shape
    channels = form_factors.shape[0]
    columns = column_map.shape[0]
    col_dev = columns // n_pw
    atoms = atom_sites.shape[1]
    vectors = blocks * slab
    rows = 2 * slab * channels
    span = 32
    while span < 2 * planes:
        span *= 2
    group = max(g for g in (1, 2, 3, 4) if planes % g == 0)
    lanes = n_pw * span
    fold_rows = col_dev * span // 128
    messages = max(1, slab * 2 * vectors // 128)
    assert grid <= 256 and slab == n_band and rows <= n_dev and lanes % 128 == 0
    assert span <= 128 and fold_rows * 128 == col_dev * span
    assert 2 * vectors <= 128 and 2 * slab * slab <= 128 and slab % messages == 0
    if columns > 512:
        column_map = column_map.reshape(n_pw, col_dev).T
    tables = host_tables(grid, planes, n_pw, span)
    cfg = (n_band, n_pw, slab, blocks, channels, planes, grid, col_dev, span, group)
    vmem = pl.BlockSpec(memory_space=pltpu.VMEM)
    smem = pl.BlockSpec(memory_space=pltpu.SMEM)
    parts = atoms // 128
    anywhere = pl.BlockSpec(memory_space=pl.ANY)
    packed = pl.pallas_call(
        functools.partial(kernel, cfg),
        out_shape=jax.ShapeDtypeStruct((6 * slab, max(waves, 128)), f32),
        in_specs=[anywhere] + [vmem] * 4 + [smem] + [vmem] * 5 + [anywhere] * 4,
        out_specs=vmem,
        scratch_shapes=[
            pltpu.VMEM((slab, n_pw, fold_rows, 128), f32),
            pltpu.VMEM((n_dev, fold_rows, 128), f32),
            pltpu.VMEM((span, columns), f32),
            pltpu.VMEM((rows, parts, 128), f32),
            pltpu.VMEM((n_dev, parts, 128), f32),
            pltpu.VMEM((parts, 128), f32),
            pltpu.VMEM((rows, parts, 128), f32),
            pltpu.VMEM((span, columns), f32),
            pltpu.VMEM((n_pw, fold_rows, 128), f32),
            pltpu.VMEM((n_dev, fold_rows, 128), f32),
            pltpu.VMEM((slab, 128), f32),
            pltpu.VMEM((messages, 128), f32),
            pltpu.VMEM((n_dev, messages, 128), f32),
            pltpu.VMEM((1, 128), f32),
            pltpu.VMEM((n_dev, 1, 128), f32),
            pltpu.VMEM((waves, atoms), bf16),
            pltpu.VMEM((waves, atoms), bf16),
            pltpu.VMEM((planes, grid, grid), f32),
            pltpu.VMEM((2, lanes, grid), bf16),
            pltpu.VMEM((2, lanes, grid), bf16),
            pltpu.VMEM((2, grid, grid), bf16),
            pltpu.VMEM((2, grid, grid), bf16),
            *[
                pltpu.VMEM(shape if columns <= 512 else (16, 128), bf16)
                for shape in (
                    (512, 6 * columns),
                    (1536, 2 * columns),
                    (group * grid, 1024),
                )
            ],
            pltpu.SemaphoreType.DMA((6,)),
            pltpu.SemaphoreType.DMA((6,)),
            pltpu.SemaphoreType.DMA((5,)),
        ],
        compiler_params=pltpu.CompilerParams(
            collective_id=0, has_side_effects=True, vmem_limit_bytes=56 * 2**20
        ),
    )(
        potential,
        basis_re,
        basis_im,
        kinetic,
        form_factors,
        channel_strength,
        sphere_map,
        column_map.reshape(1, columns),
        atom_sites,
        *tables,
    )
    next_re, next_im, coef_re, coef_im, chol_re, chol_im = pl.pallas_call(
        functools.partial(finish, slab, blocks),
        out_shape=[
            jax.ShapeDtypeStruct((slab, 1, waves), f32),
            jax.ShapeDtypeStruct((slab, 1, waves), f32),
            jax.ShapeDtypeStruct((slab, slab, blocks), f32),
            jax.ShapeDtypeStruct((slab, slab, blocks), f32),
            jax.ShapeDtypeStruct((slab, slab), f32),
            jax.ShapeDtypeStruct((slab, slab), f32),
        ],
        in_specs=[vmem],
        out_specs=[vmem] * 6,
    )(packed)
    return (
        next_re,
        next_im,
        coef_re.transpose(2, 0, 1),
        coef_im.transpose(2, 0, 1),
        chol_re,
        chol_im,
    )


def solution(mesh):
    return jax.shard_map(
        body,
        mesh=mesh,
        in_specs=(
            P(None, None, "band", "pw"),
            P(None, None, "band", "pw"),
            P("pw", None, None),
            P(None, "pw"),
            P(None, None, "pw"),
            P(),
            P(None, "pw"),
            P(),
            P(),
        ),
        out_specs=(P(None, "band", "pw"), P(None, "band", "pw"), P(), P(), P(), P()),
        check_vma=False,
    )
```

```python
import functools
import math

import jax
import jax.numpy as jnp
import numpy as np
from jax import lax
from jax.experimental import pallas as pl
from jax.experimental.pallas import tpu as pltpu
from jax.sharding import PartitionSpec as P

f32 = jnp.float32
bf16 = jnp.bfloat16
NN = (((1,), (0,)), ((), ()))
NT = (((1,), (1,)), ((), ()))
TN = (((0,), (0,)), ((), ()))


def dot(left, right, dims):
    return lax.dot_general(left, right, dims, preferred_element_type=f32)


def exact_dot(left, right, dims):
    return lax.dot_general(
        left, right, dims, precision=lax.Precision.HIGHEST, preferred_element_type=f32
    )


def halves(value):
    high = value.astype(bf16)
    return high, (value - high.astype(f32)).astype(bf16)


def dot_split(value, table_high, table_low, dims):
    high, low = halves(value)
    return (
        dot(high, table_high, dims) + dot(low, table_high, dims) + dot(high, table_low, dims)
    )


def table_halves(table):
    table = np.asarray(table, np.float32)
    high = table.astype(jnp.bfloat16)
    low = (table - high.astype(np.float32)).astype(jnp.bfloat16)
    return jnp.asarray(high), jnp.asarray(low)


def host_tables(grid, planes, wave_groups, span):
    ticks = np.arange(grid)
    angle = (ticks[:, None] * ticks[None, :] % grid) * (2.0 * math.pi / grid)
    cos, sin = np.cos(angle), np.sin(angle)
    lanes = wave_groups * span
    spread = np.zeros((2, grid, wave_groups, 2, span // 2))
    split_cos = cos.reshape(grid, wave_groups, planes)
    split_sin = sin.reshape(grid, wave_groups, planes)
    spread[0, :, :, 0, :planes] = split_cos
    spread[0, :, :, 1, :planes] = split_sin
    spread[1, :, :, 0, :planes] = -split_sin
    spread[1, :, :, 1, :planes] = split_cos
    spread = spread.reshape(2, grid, lanes)
    back = np.zeros((2, wave_groups, 2, span // 2, grid))
    scale = 1.0 / float(grid) ** 3
    rows_cos = cos.reshape(wave_groups, planes, grid) * scale
    rows_sin = sin.reshape(wave_groups, planes, grid) * scale
    back[0, :, 0, :planes] = rows_cos
    back[0, :, 1, :planes] = rows_sin
    back[1, :, 0, :planes] = -rows_sin
    back[1, :, 1, :planes] = rows_cos
    back = back.reshape(2, lanes, grid)
    return (
        *table_halves(spread),
        *table_halves(back),
        *table_halves(np.stack([cos, sin])),
    )


def cos_sin_192(turns, grid):
    quarter = grid // 4
    step = jnp.floor(turns * (1.0 / quarter) + 0.5)
    rest = turns - step * quarter
    x = rest * (2.0 * math.pi / grid)
    x2 = x * x
    sine = x + x * x2 * (
        -1.6666654611e-1 + x2 * (8.3321608736e-3 + x2 * -1.9515295891e-4)
    )
    cosine = (
        1.0
        - 0.5 * x2
        + x2 * x2 * (4.166664568298827e-2 + x2 * (-1.388731625493765e-3 + x2 * 2.443315711809948e-5))
    )
    count = step.astype(jnp.int32)
    odd = (count & 1) == 1
    flip_cos = ((count + 1) & 2) == 2
    flip_sin = (count & 2) == 2
    out_cos = jnp.where(odd, sine, cosine)
    out_sin = jnp.where(odd, cosine, sine)
    return (
        jnp.where(flip_cos, -out_cos, out_cos),
        jnp.where(flip_sin, -out_sin, out_sin),
    )


def kernel(
    cfg,
    pot_ref,
    basis_re_ref,
    basis_im_ref,
    kin_ref,
    form_ref,
    strength_ref,
    sphere_ref,
    cmap_ref,
    sites_ref,
    t1h_ref,
    t1l_ref,
    f2h_ref,
    f2l_ref,
    dh_ref,
    dl_ref,
    packed_ref,
    y1_buf,
    col_buf,
    col_s,
    ps_send,
    ps_recv,
    sc_send,
    sc_buf,
    out_s,
    out_send,
    out_buf,
    row_pad,
    co_send,
    co_buf,
    gr_send,
    gr_buf,
    phase_cos,
    phase_sin,
    pot_buf,
    f2h_buf,
    f2l_buf,
    dh_buf,
    dl_buf,
    fwd_table,
    back_table,
    back_left,
    send_sem,
    recv_sem,
    load_sem,
):
    n_band, n_pw, slab, blocks, channels, planes, grid, col_dev, span, group = cfg
    n_dev = n_band * n_pw
    vectors = blocks * slab
    columns = n_pw * col_dev
    per_tile = 128 // span
    tiles = n_pw * span // 128
    fold_rows = col_dev // per_tile
    piece = fold_rows * n_pw
    atoms = sites_ref.shape[1]
    rows = 2 * slab * channels
    half_rows = slab * channels
    waves = kin_ref.shape[1]
    total_waves = n_dev * waves
    root_waves = math.sqrt(total_waves)
    s = lax.axis_index("band")
    q = lax.axis_index("pw")
    me = s * n_pw + q

    def wrap(value, size):
        return jnp.where(value >= size, value - size, value)

    def others(act):
        for turn in reversed(range(n_band)):
            band = wrap(s + turn, n_band)

            def one(k, carry):
                act(band, wrap(q + k, n_pw))
                return carry

            if n_dev <= 64:
                for k in sorted(range(1, n_pw), key=lambda k: -min(k, n_pw - k)):
                    one(k, 0)
            else:
                lax.fori_loop(1, n_pw, one, 0)
            if turn:
                act(band, q)

    barrier = pltpu.get_barrier_semaphore()
    others(
        lambda band, pw: pl.semaphore_signal(
            barrier, inc=1, device_id=(band, pw), device_id_type=pl.DeviceIdType.MESH
        )
    )
    loads = [
        pltpu.make_async_copy(source, target, load_sem.at[i])
        for i, (source, target) in enumerate(
            [
                (dh_ref, dh_buf),
                (dl_ref, dl_buf),
                (pot_ref, pot_buf),
                (f2h_ref, f2h_buf),
                (f2l_ref, f2l_buf),
            ]
        )
    ]
    for load in loads:
        load.start()

    def push(source, target, sem, limit=n_dev):
        def one(band, pw):
            def go():
                pltpu.make_async_remote_copy(
                    src_ref=source(band, pw),
                    dst_ref=target,
                    send_sem=send_sem.at[sem],
                    recv_sem=recv_sem.at[sem],
                    device_id=(band, pw),
                    device_id_type=pl.DeviceIdType.MESH,
                ).start()

            if limit < n_dev:
                pl.when(band * n_pw + pw < limit)(go)
            else:
                go()

        others(one)

    def take(buf, sem, count):
        view = buf.at[pl.ds(0, count)]
        pltpu.make_async_copy(view, view, sem).wait()

    cells = sphere_ref[pl.ds(s, 1), :].astype(f32)
    depth = jnp.floor((cells + 0.5) * (1.0 / col_dev))
    column = cells - depth * col_dev
    mask = (
        lax.broadcasted_iota(jnp.int32, (col_dev, waves), 0) == column.astype(jnp.int32)
    ).astype(f32)
    one_hot = jnp.where(
        lax.broadcasted_iota(jnp.int32, (grid, waves), 0) == depth.astype(jnp.int32), 1.0, 0.0
    ).astype(bf16)
    flat_re, flat_im = [
        jnp.concatenate([ref[j, k] for j in range(blocks) for k in range(slab)], 0)
        for ref in (basis_re_ref, basis_im_ref)
    ]
    psi_re = flat_re[vectors - slab :]
    psi_im = flat_im[vectors - slab :]
    placed = jnp.concatenate(
        [mask * psi_re[b : b + 1] for b in range(slab)]
        + [mask * psi_im[b : b + 1] for b in range(slab)],
        0,
    )
    high, low = halves(placed)
    field = dot(high, one_hot, NT) + dot(low, one_hot, NT)
    half = slab * col_dev
    spread = dot_split(field[:half], t1h_ref[0], t1l_ref[0], NN) + dot_split(
        field[half:], t1h_ref[1], t1l_ref[1], NN
    )
    block = lax.broadcasted_iota(jnp.int32, (col_dev, 128), 1) // span
    diagonal = lax.broadcasted_iota(jnp.int32, (col_dev, 128), 0) // fold_rows == block

    def turned(tile, turn):
        shift = turn % per_tile * span
        return pltpu.roll(tile, shift, 1) if shift else tile

    for b in range(slab):
        for t in range(tiles):
            tile = spread[b * col_dev : (b + 1) * col_dev, t * 128 : (t + 1) * 128]
            turns = [turned(tile, d) for d in range(per_tile)]
            for j in range(per_tile):
                message = turns[-j % per_tile]
                for g in range(1, per_tile):
                    message = jnp.where(block == g, turns[(g - j) % per_tile], message)
                message = jnp.where(diagonal, message, 0.0)
                shift = col_dev // 2
                while shift >= fold_rows:
                    message = message + pltpu.roll(message, shift, 0)
                    shift //= 2
                y1_buf[b, t * per_tile + j] = message[:fold_rows]

    pl.semaphore_wait(barrier, n_dev - 1)
    push(
        lambda band, pw: y1_buf.at[band, pw],
        col_buf.at[me],
        0,
    )
    col_buf[me] = y1_buf[s, q]

    col_x = cmap_ref[...].astype(f32)
    all_x = jnp.floor((col_x + 0.5) * (1.0 / grid))
    all_y = col_x - all_x * grid
    if columns <= 512:
        spot = lax.broadcasted_iota(jnp.int32, (columns, columns), 1)
        moved = lax.broadcasted_iota(jnp.int32, (columns, columns), 0) == (
            lax.rem(spot, n_pw) * col_dev + spot // n_pw
        )
        both = jnp.concatenate([all_x, all_y, jnp.zeros((6, columns), f32)], 0)
        both = dot(both.astype(bf16), jnp.where(moved, 1.0, 0.0).astype(bf16), NN)
        all_x, all_y = both[0:1], both[1:2]
    own = lax.broadcasted_iota(jnp.int32, (col_dev, columns), 1) == (
        lax.broadcasted_iota(jnp.int32, (col_dev, columns), 0) * n_pw + q
    )
    own_x = jnp.sum(jnp.where(own, all_x, 0.0), 1, keepdims=True)
    own_y = jnp.sum(jnp.where(own, all_y, 0.0), 1, keepdims=True)
    wave_x = jnp.sum(mask * own_x, 0, keepdims=True)
    wave_y = jnp.sum(mask * own_y, 0, keepdims=True)
    places = jnp.concatenate([depth, wave_x, wave_y, jnp.zeros((5, waves), f32)], 0)
    sites = jnp.concatenate([sites_ref[...].astype(f32), jnp.zeros((5, atoms), f32)], 0)
    turns = dot(places.T.astype(bf16), sites.astype(bf16), NN)
    cosine, sine = cos_sin_192(turns, grid)
    phase_cos[...] = cosine.astype(bf16)
    phase_sin[...] = sine.astype(bf16)
    form = form_ref[:, pl.ds(s, 1), :].reshape(channels, waves)
    weighted = jnp.concatenate(
        [form * psi_re[b : b + 1] for b in range(slab)]
        + [form * psi_im[b : b + 1] for b in range(slab)],
        0,
    ).astype(bf16)
    with_cos = dot(weighted, phase_cos[...], NN)
    with_sin = dot(weighted, phase_sin[...], NN)
    sums = jnp.concatenate(
        [
            with_cos[:half_rows] - with_sin[half_rows:],
            with_sin[:half_rows] + with_cos[half_rows:],
        ],
        0,
    )
    parts = atoms // 128
    for t in range(parts):
        ps_send[:, t, :] = sums[:, t * 128 : (t + 1) * 128]
    push(lambda band, pw: ps_send.at[band * n_pw + pw], ps_recv.at[me], 1, rows)

    loads[0].wait()
    loads[1].wait()

    def at_columns(position):
        ticks = lax.broadcasted_iota(jnp.int32, (grid, columns), 0)
        chosen = jnp.where(ticks == position.astype(jnp.int32), 1.0, 0.0).astype(bf16)
        return [dot(table[i], chosen, NN) for table in (dh_buf, dl_buf) for i in (0, 1)]

    xch, xsh, xcl, xsl = at_columns(all_x)
    x_cos = xch + xcl
    x_sin = xsh + xsl
    ych, ysh, ycl, ysl = [part.astype(bf16) for part in at_columns(all_y)]
    joined = columns <= 512
    mre_high = jnp.concatenate([ych, -ysh], 1)
    mre_low = jnp.concatenate([ycl, -ysl], 1)
    mim_high = jnp.concatenate([ysh, ych], 1)
    mim_low = jnp.concatenate([ysl, ycl], 1)

    if joined:
        gap = jnp.zeros((256 - grid, 2 * columns), bf16)
        high = jnp.concatenate([mre_high, gap, mim_high, gap], 0)
        low = jnp.concatenate([mre_low, gap, mim_low, gap], 0)
        fwd_table[...] = jnp.concatenate([high, high, low], 1)
        back_table[...] = jnp.concatenate(
            [mre_high, gap, mre_high, gap, mim_high, gap, mim_high, gap, low], 0
        )
        back_left[...] = jnp.zeros_like(back_left)
    out_s[...] = jnp.zeros_like(out_s)

    take(col_buf, recv_sem.at[0], n_dev - 1)
    gathered = []
    for r in range(fold_rows):
        line = col_buf[:, r, :]
        total = line[0:n_pw]
        for b in range(1, n_band):
            total = total + line[b * n_pw : (b + 1) * n_pw]
        gathered.append(total)
    gathered = jnp.concatenate(gathered, 0).T
    col_s[...] = jnp.concatenate(
        [gathered[g * span : (g + 1) * span] for g in range(per_tile)], 1
    )

    loads[2].wait()

    def some_planes(step, carry):
        first = step * group
        mixed = []
        for i in range(group):
            part_re = col_s[pl.ds(first + i, 1), :]
            part_im = col_s[pl.ds(span // 2 + first + i, 1), :]
            mixed.append(
                jnp.concatenate(
                    [x_cos * part_re - x_sin * part_im, x_cos * part_im + x_sin * part_re], 1
                )
            )
        mixed = jnp.concatenate(mixed, 0)
        weight = pot_buf[pl.ds(first, group)].reshape(group * grid, grid)
        if joined:
            high, low = halves(mixed)
            field = dot(jnp.concatenate([high, low, high], 1), fwd_table[...], NT)
            re_high, re_low = halves(field[:, :grid] * weight)
            im_high, im_low = halves(field[:, 256 : 256 + grid] * weight)
            for i, part in enumerate((re_low, re_high, im_high, im_low)):
                back_left[:, i * 256 : i * 256 + grid] = part
            back = dot(back_left[...], back_table[0:1024], NN) + dot(
                back_left[:, 256:768], back_table[1024:1536], NN
            )
        else:
            field_re = dot_split(mixed, mre_high, mre_low, NT)
            field_im = dot_split(mixed, mim_high, mim_low, NT)
            back = dot_split(field_re * weight, mre_high, mre_low, NN) + dot_split(
                field_im * weight, mim_high, mim_low, NN
            )
        for i in range(group):
            back_re = back[i * grid : (i + 1) * grid, :columns]
            back_im = back[i * grid : (i + 1) * grid, columns:]
            out_s[pl.ds(first + i, 1), :] = jnp.sum(
                x_cos * back_re + x_sin * back_im, 0, keepdims=True
            )
            out_s[pl.ds(span // 2 + first + i, 1), :] = jnp.sum(
                x_cos * back_im - x_sin * back_re, 0, keepdims=True
            )
        return carry

    some_planes(0, 0)

    def own_row():
        ps_recv[me] = ps_send[me]
        take(ps_recv, recv_sem.at[1], n_dev - 1)
        total = jnp.sum(ps_recv[...], 0)
        strength = strength_ref[lax.rem(me, channels)]
        sc_send[...] = strength * (total * (1.0 / root_waves)) * (1.0 / root_waves)
        sc_buf[me] = sc_send[...]
        push(lambda band, pw: sc_send, sc_buf.at[me], 2)

    if rows < n_dev:
        pl.when(me < rows)(own_row)
    else:
        own_row()

    if planes > group:
        lax.fori_loop(1, planes // group, some_planes, 0)
    flipped = out_s[...]
    flipped = jnp.concatenate(
        [flipped[:, g * piece : (g + 1) * piece] for g in range(per_tile)], 0
    ).T
    for r in range(fold_rows):
        out_send[:, r, :] = flipped[r * n_pw : (r + 1) * n_pw]
    push(lambda band, pw: out_send.at[pw], out_buf.at[me], 3)
    out_buf[me] = out_send[q]

    if rows < n_dev:
        pl.when(me < rows)(lambda: take(sc_buf, recv_sem.at[2], rows - 1))
        pl.when(me >= rows)(lambda: take(sc_buf, recv_sem.at[2], rows))
    else:
        take(sc_buf, recv_sem.at[2], rows - 1)
    scaled = jnp.concatenate([sc_buf[:, t, :] for t in range(parts)], 1)
    scaled_re = scaled[:half_rows]
    scaled_im = scaled[half_rows:]
    near = dot(
        jnp.concatenate([scaled_re, scaled_im], 0).astype(bf16), phase_cos[...], NT
    ) + dot(jnp.concatenate([scaled_im, -scaled_re], 0).astype(bf16), phase_sin[...], NT)
    near = [
        jnp.sum(form * near[i * channels : (i + 1) * channels], 0, keepdims=True)
        for i in range(2 * slab)
    ]
    psi_all = jnp.concatenate([psi_re, psi_im], 0)
    image = kin_ref[pl.ds(s, 1), :] * psi_all + jnp.concatenate(near, 0)

    loads[3].wait()
    loads[4].wait()
    take(out_buf, recv_sem.at[3], n_dev - 1)
    lines = []
    for b in range(slab):
        line = []
        for t in range(tiles):
            begin = b * n_pw + t * per_tile
            wide = [
                jnp.concatenate([out_buf[begin + j]] * per_tile, 0) for j in range(per_tile)
            ]
            tile = None
            for d in range(per_tile):
                part = wide[d]
                for g in range(1, per_tile):
                    part = jnp.where(block == g, wide[(g + d) % per_tile], part)
                part = turned(jnp.where(diagonal, part, 0.0), d)
                tile = part if tile is None else tile + part
            line.append(tile)
        lines.append(jnp.concatenate(line, 1))
    lines = jnp.concatenate(lines, 0)
    high, low = halves(lines)
    depths = [
        dot(high, f2h_buf[i], NN) + dot(low, f2h_buf[i], NN) + dot(high, f2l_buf[i], NN)
        for i in (0, 1)
    ]
    high, low = halves(jnp.concatenate(depths, 0))
    read = dot(high, one_hot, NN) + dot(low, one_hot, NN)
    local = [
        jnp.sum(mask * read[i * col_dev : (i + 1) * col_dev], 0, keepdims=True)
        for i in range(2 * slab)
    ]
    image = image + jnp.concatenate(local, 0)

    def doubled(wave):
        first, second = wave[:slab], wave[slab:]
        return jnp.concatenate(
            [
                jnp.concatenate([first, second], 1),
                jnp.concatenate([second, -first], 1),
            ],
            0,
        )

    span_rows = jnp.concatenate([flat_re, flat_im], 0)
    span_double = jnp.concatenate(
        [jnp.concatenate([flat_re, flat_im], 1), jnp.concatenate([flat_im, -flat_re], 1)], 0
    )
    count = 2 * slab
    wide = 2 * vectors
    folds = slab // co_send.shape[0]
    row_pad[...] = jnp.zeros_like(row_pad)
    row_pad[:, 0:wide] = exact_dot(doubled(image)[:slab], span_double, NT) * (
        1.0 / total_waves
    )
    for m in range(slab // folds):
        line = row_pad[m * folds : m * folds + 1, :]
        for i in range(1, folds):
            line = line + pltpu.roll(row_pad[m * folds + i : m * folds + i + 1, :], i * wide, 1)
        co_send[m : m + 1, :] = line
    push(lambda band, pw: co_send, co_buf.at[me], 4)
    co_buf[me] = co_send[...]
    take(co_buf, recv_sem.at[4], n_dev - 1)
    coef = jnp.sum(co_buf[...], 0)
    top = []
    for b in range(slab):
        line = coef[b // folds : b // folds + 1]
        if b % folds:
            line = pltpu.roll(line, 128 - b % folds * wide, 1)
        top.append(line[:, :wide])
    top = jnp.concatenate(top, 0)
    coef = jnp.concatenate(
        [top, jnp.concatenate([-top[:, vectors:], top[:, :vectors]], 1)], 0
    )
    residue = image - exact_dot(coef, span_rows, NN)

    residue_double = doubled(residue)
    row_pad[...] = jnp.zeros_like(row_pad)
    row_pad[:, 0:count] = exact_dot(residue_double[:slab], residue_double, NT) * (
        1.0 / total_waves
    )
    line = row_pad[0:1, :]
    for r in range(1, slab):
        line = line + pltpu.roll(row_pad[r : r + 1, :], r * count, 1)
    gr_send[...] = line
    push(lambda band, pw: gr_send, gr_buf.at[me], 5)
    gr_buf[me] = gr_send[...]

    packed_ref[0:count] = residue
    lane_out = lax.broadcasted_iota(jnp.int32, (vectors, vectors), 0)
    lane_in = lax.broadcasted_iota(jnp.int32, (vectors, vectors), 1)
    order = (lane_in == lax.rem(lane_out, blocks) * slab + lane_out // blocks).astype(f32)
    packed_ref[count : 2 * count, 0:vectors] = exact_dot(coef[:, :vectors], order, NT)
    take(gr_buf, recv_sem.at[5], n_dev - 1)
    gram = jnp.sum(gr_buf[...], 0)
    for r in range(slab):
        packed_ref[2 * count + r : 2 * count + r + 1, 0:128] = (
            pltpu.roll(gram, 128 - r * count, 1) if r else gram
        )

    take(col_buf, send_sem.at[0], n_dev - 1)
    if rows < n_dev:
        pl.when(me < rows)(lambda: take(ps_recv, send_sem.at[1], rows - 1))
        pl.when(me >= rows)(lambda: take(ps_recv, send_sem.at[1], rows))
        pl.when(me < rows)(lambda: take(ps_recv, send_sem.at[2], n_dev - 1))
    else:
        take(ps_recv, send_sem.at[1], rows - 1)
        take(ps_recv, send_sem.at[2], n_dev - 1)
    take(out_buf, send_sem.at[3], n_dev - 1)
    take(co_buf, send_sem.at[4], n_dev - 1)
    take(gr_buf, send_sem.at[5], n_dev - 1)


def finish(
    slab,
    blocks,
    packed_ref,
    next_re_ref,
    next_im_ref,
    coef_re_ref,
    coef_im_ref,
    chol_re_ref,
    chol_im_ref,
):
    count = 2 * slab
    vectors = blocks * slab
    residue = packed_ref[0:count]
    gram = packed_ref[2 * count : 3 * count, 0:128]
    for part, ref in ((0, coef_re_ref), (slab, coef_im_ref)):
        line = packed_ref[count + part : count + part + slab, 0:vectors]
        for k in range(slab):
            ref[k] = line[:, k * blocks : (k + 1) * blocks]

    lane = lax.broadcasted_iota(jnp.int32, (1, gram.shape[1]), 1)

    def entry(row, index):
        return jnp.sum(jnp.where(lane == index, row, 0.0), 1, keepdims=True)

    def moved(row):
        return pltpu.roll(row, gram.shape[1] - slab, 1)

    upper = []
    for r in range(slab):
        total_re = gram[r : r + 1]
        total_im = moved(gram[r : r + 1])
        for up_re, up_im in upper:
            a_re, a_im = entry(up_re, r), entry(up_im, r)
            total_re, total_im = (
                total_re - (a_re * up_re + a_im * up_im),
                total_im - (a_re * up_im - a_im * up_re),
            )
        pivot = jnp.sqrt(entry(total_re, r))
        ok = lane < slab
        upper.append(
            (
                jnp.where((lane >= r) & ok, total_re / pivot, 0.0),
                jnp.where((lane > r) & ok, total_im / pivot, 0.0),
            )
        )
    chol_re_ref[...] = jnp.concatenate([u[0] for u in upper], 0)[:, :slab]
    chol_im_ref[...] = jnp.concatenate([u[1] for u in upper], 0)[:, :slab]
    solved = []
    for e in range(slab):
        row_re = residue[e : e + 1]
        row_im = residue[slab + e : slab + e + 1]
        for b in range(e):
            r_re, r_im = entry(upper[b][0], e), entry(upper[b][1], e)
            row_re, row_im = (
                row_re - (solved[b][0] * r_re - solved[b][1] * r_im),
                row_im - (solved[b][0] * r_im + solved[b][1] * r_re),
            )
        inverse = 1.0 / entry(upper[e][0], e)
        solved.append((row_re * inverse, row_im * inverse))
    for e in range(slab):
        next_re_ref[e] = solved[e][0]
        next_im_ref[e] = solved[e][1]


def body(
    basis_re,
    basis_im,
    potential,
    kinetic,
    form_factors,
    channel_strength,
    sphere_map,
    column_map,
    atom_sites,
):
    blocks, slab, _, waves = basis_re.shape
    n_band = lax.axis_size("band")
    n_pw = lax.axis_size("pw")
    n_dev = n_band * n_pw
    planes, grid, _ = potential.shape
    channels = form_factors.shape[0]
    columns = column_map.shape[0]
    col_dev = columns // n_pw
    atoms = atom_sites.shape[1]
    vectors = blocks * slab
    rows = 2 * slab * channels
    span = 32
    while span < 2 * planes:
        span *= 2
    group = max(g for g in (1, 2, 3, 4) if planes % g == 0)
    lanes = n_pw * span
    fold_rows = col_dev * span // 128
    messages = max(1, slab * 2 * vectors // 128)
    assert grid <= 256 and slab == n_band and rows <= n_dev and lanes % 128 == 0
    assert span <= 128 and fold_rows * 128 == col_dev * span
    assert 2 * vectors <= 128 and 2 * slab * slab <= 128 and slab % messages == 0
    if columns > 512:
        column_map = column_map.reshape(n_pw, col_dev).T
    tables = host_tables(grid, planes, n_pw, span)
    cfg = (n_band, n_pw, slab, blocks, channels, planes, grid, col_dev, span, group)
    vmem = pl.BlockSpec(memory_space=pltpu.VMEM)
    smem = pl.BlockSpec(memory_space=pltpu.SMEM)
    parts = atoms // 128
    anywhere = pl.BlockSpec(memory_space=pl.ANY)
    packed = pl.pallas_call(
        functools.partial(kernel, cfg),
        out_shape=jax.ShapeDtypeStruct((6 * slab, max(waves, 128)), f32),
        in_specs=[anywhere] + [vmem] * 4 + [smem] + [vmem] * 5 + [anywhere] * 4,
        out_specs=vmem,
        scratch_shapes=[
            pltpu.VMEM((slab, n_pw, fold_rows, 128), f32),
            pltpu.VMEM((n_dev, fold_rows, 128), f32),
            pltpu.VMEM((span, columns), f32),
            pltpu.VMEM((rows, parts, 128), f32),
            pltpu.VMEM((n_dev, parts, 128), f32),
            pltpu.VMEM((parts, 128), f32),
            pltpu.VMEM((rows, parts, 128), f32),
            pltpu.VMEM((span, columns), f32),
            pltpu.VMEM((n_pw, fold_rows, 128), f32),
            pltpu.VMEM((n_dev, fold_rows, 128), f32),
            pltpu.VMEM((slab, 128), f32),
            pltpu.VMEM((messages, 128), f32),
            pltpu.VMEM((n_dev, messages, 128), f32),
            pltpu.VMEM((1, 128), f32),
            pltpu.VMEM((n_dev, 1, 128), f32),
            pltpu.VMEM((waves, atoms), bf16),
            pltpu.VMEM((waves, atoms), bf16),
            pltpu.VMEM((planes, grid, grid), f32),
            pltpu.VMEM((2, lanes, grid), bf16),
            pltpu.VMEM((2, lanes, grid), bf16),
            pltpu.VMEM((2, grid, grid), bf16),
            pltpu.VMEM((2, grid, grid), bf16),
            *[
                pltpu.VMEM(shape if columns <= 512 else (16, 128), bf16)
                for shape in (
                    (512, 6 * columns),
                    (1536, 2 * columns),
                    (group * grid, 1024),
                )
            ],
            pltpu.SemaphoreType.DMA((6,)),
            pltpu.SemaphoreType.DMA((6,)),
            pltpu.SemaphoreType.DMA((5,)),
        ],
        compiler_params=pltpu.CompilerParams(
            collective_id=0, has_side_effects=True, vmem_limit_bytes=56 * 2**20
        ),
    )(
        potential,
        basis_re,
        basis_im,
        kinetic,
        form_factors,
        channel_strength,
        sphere_map,
        column_map.reshape(1, columns),
        atom_sites,
        *tables,
    )
    next_re, next_im, coef_re, coef_im, chol_re, chol_im = pl.pallas_call(
        functools.partial(finish, slab, blocks),
        out_shape=[
            jax.ShapeDtypeStruct((slab, 1, waves), f32),
            jax.ShapeDtypeStruct((slab, 1, waves), f32),
            jax.ShapeDtypeStruct((slab, slab, blocks), f32),
            jax.ShapeDtypeStruct((slab, slab, blocks), f32),
            jax.ShapeDtypeStruct((slab, slab), f32),
            jax.ShapeDtypeStruct((slab, slab), f32),
        ],
        in_specs=[vmem],
        out_specs=[vmem] * 6,
    )(packed)
    return (
        next_re,
        next_im,
        coef_re.transpose(2, 0, 1),
        coef_im.transpose(2, 0, 1),
        chol_re,
        chol_im,
    )


def solution(mesh):
    return jax.shard_map(
        body,
        mesh=mesh,
        in_specs=(
            P(None, None, "band", "pw"),
            P(None, None, "band", "pw"),
            P("pw", None, None),
            P(None, "pw"),
            P(None, None, "pw"),
            P(),
            P(None, "pw"),
            P(),
            P(),
        ),
        out_specs=(P(None, "band", "pw"), P(None, "band", "pw"), P(), P(), P(), P()),
        check_vma=False,
    )
```
